256 devices in a mesh: dp: 8 (over z_lo, y), tensor: 32 (over z_hi, x, core).
Axes of the slice: x: 4, y: 4, z: 8 (z_hi: 4, z_lo: 2; z = z_hi * 2 + z_lo), core: 2. Of those that a mesh axis runs over, the one named last changes fastest.
Arguments:
- old_master: float32 [32, 8, 128, 2048], P('tensor', 'dp'), may hold values from -6 to 6
- old_moment: float32 [32, 8, 128, 2048], P('tensor', 'dp'), may hold values from -3 to 3
- old_second: float32 [32, 8, 128, 2048], P('tensor', 'dp'), may hold values from 0.25 to 4
- tokens_in: bfloat16 [4096, 4096], P('dp'), may hold values from -6 to 6
- upstream: bfloat16 [4096, 16384], P('dp', 'tensor'), may hold values from -6 to 6
- counts: int32 [8], replicated, may hold values from 128 to 512, as said below
- old_map: int32 [32], replicated, may hold values from 0 to 31, each once
- new_map: int32 [32], replicated, may hold values from 0 to 31, each once
Outputs:
- new_master: float32 [32, 8, 256, 1024], P('tensor', 'dp')
- new_moment: float32 [32, 8, 256, 1024], P('tensor', 'dp')
- new_second: float32 [32, 8, 256, 1024], P('tensor', 'dp')
- input_grad: bfloat16 [4096, 4096], P('dp', 'tensor')
The draws below stay inside these ranges and needn't reach their ends.
Inputs may be any that keep to these rules, and one draw needn't show every extreme that they name: counts[g] tokens of data group g carry loss, the rest are padding; some group is full in every draw. `old_map`: a permutation of the tensor indices. `new_map`: a permutation of the tensor indices.
All inputs are finite; a program needn't handle non-finite values.
Results may differ from the reference program's by a relative error of at most 0.0049.
Values may be sent and summed in bfloat16 or wider, within the bound.
A program may use at most 128 MiB of HBM per device.

```python
import math
import jax
import jax.numpy as jnp

D = 4096
FW = 16384
TOK = 512
TOKENS = 4096
R_OLD = 4
R_NEW = 2
RO = 128
RN = 256
CO = 2048
CN = 1024
N_DP = 8
N_TENSOR = 32


def draw_counts(key, part):
    key = jax.random.fold_in(key, 11)
    first, second = jax.random.split(key)
    values = jax.random.randint(first, (N_DP,), TOK // 4, TOK + 1)
    chosen = jax.random.randint(second, (), 0, N_DP)
    return jnp.where(jnp.arange(N_DP) == chosen, TOK, values).astype(jnp.int32)


def steps_of(key, dims, shards, least, high):
    def one(axis_at, shards_of):
        heights = jax.random.uniform(jax.random.fold_in(jax.random.fold_in(key, 6), axis_at), (shards_of,), jnp.float32, least / len(shards), high / len(shards))
        return jnp.repeat(jnp.exp(heights), dims[axis_at] // shards_of).reshape((-1,) + (1,) * (len(dims) - axis_at - 1))

    factor_of = one(*shards[0])
    for cut in shards[1:]:
        factor_of = factor_of * one(*cut)
    return factor_of


def centred(own_key, shape, width, bound, pieces=(), kind=jnp.bfloat16):
    result = width * jax.random.normal(own_key, shape, jnp.float32)
    if pieces:
        result = result * steps_of(own_key, shape, pieces, -0.22, 0.18)
    return jnp.clip(result, -bound, bound).astype(kind)


def setup_inputs(seed: int = 0) -> dict:
    seeds = jax.random.split(jax.random.key(seed), 9)
    old_master = centred(seeds[0], (N_TENSOR, N_DP, RO, CO), 1.0, 6.0, ((0, 32), (1, 8)), jnp.float32)
    old_moment = centred(seeds[1], (N_TENSOR, N_DP, RO, CO), 0.5, 3.0, ((0, 32), (1, 8)), jnp.float32)
    old_second = jnp.clip(jnp.exp(math.log(4.0) - 2.7725887 * jax.random.uniform(seeds[2], (N_TENSOR, N_DP, RO, CO), jnp.float32) ** steps_of(seeds[2], (N_TENSOR, N_DP, RO, CO), ((0, 32), (1, 8)), -0.2, 0.2)), 0.25, 4.0)
    tokens_in = centred(seeds[3], (TOKENS, D), 1.0, 6.0, ((0, 8),))
    upstream = centred(seeds[4], (TOKENS, FW), 1.0, 6.0, ((0, 8), (1, 32)))
    counts = draw_counts(jax.random.fold_in(seeds[8], 71), 0)
    old_map = jax.random.permutation(seeds[6], N_TENSOR).astype(jnp.int32)
    new_map = jax.random.permutation(seeds[7], N_TENSOR).astype(jnp.int32)
    return dict(old_master=old_master, old_moment=old_moment, old_second=old_second, tokens_in=tokens_in, upstream=upstream, counts=counts, old_map=old_map, new_map=new_map)


beta_first = 0.9
beta_second = 0.95
learn_rate = 0.05
decay_rate = 0.1
epsilon = 1e-08

def reference(old_master, old_moment, old_second, tokens_in, upstream, counts, old_map, new_map):
    shard_ids = jnp.arange(N_TENSOR, dtype=jnp.int32)
    inverse = jnp.zeros((N_TENSOR,), jnp.int32).at[old_map].set(shard_ids)

    def assemble(stored):
        ordered = stored[inverse].reshape(8, R_OLD, N_DP, RO, CO)
        return ordered.transpose(2, 1, 3, 0, 4).reshape(D, FW)

    def divide(whole):
        parts = whole.reshape(N_DP, R_NEW, RN, 16, CN).transpose(3, 1, 0, 2, 4)
        return parts.reshape(N_TENSOR, N_DP, RN, CN)[new_map]
    scale = float(D) ** (-0.5)
    position = jnp.arange(TOKENS, dtype=jnp.int32)
    owner = position // TOK
    live = position % TOK < counts[owner]
    masked = jnp.where(live[:, None], upstream, jnp.zeros_like(upstream))
    grad = jnp.dot(tokens_in.T, masked, preferred_element_type=jnp.float32) * scale
    master = assemble(old_master)
    weights = master.astype(jnp.bfloat16)
    input_grad = (jnp.dot(masked, weights.T, preferred_element_type=jnp.float32) * scale).astype(jnp.bfloat16)
    moment = beta_first * assemble(old_moment) + (1.0 - beta_first) * grad
    second = beta_second * assemble(old_second) + (1.0 - beta_second) * grad * grad
    fix_first = 1.0 - beta_first ** 10
    fix_second = 1.0 - beta_second ** 10
    update = moment / fix_first / (jnp.sqrt(second / fix_second) + epsilon) + decay_rate * master
    updated = master - learn_rate * update
    return (divide(updated), divide(moment), divide(second), input_grad)
```

```python
import jax
import jax.numpy as jnp
from jax import lax
from jax.experimental import pallas as pl
from jax.experimental.pallas import tpu as pltpu
from jax.sharding import PartitionSpec as P

beta_first = 0.9
beta_second = 0.95
learn_rate = 0.05
decay_rate = 0.1
epsilon = 1e-08

BF = jnp.bfloat16
F32 = jnp.float32
NT = (((1,), (1,)), ((), ()))


def kernel(
    inv_ref, new_ref, cnt_ref, om_ref, oo_ref, os_ref, tok_ref, up_ref,
    out_ref, ig_ref,
    old, tok, send1, spread_a, spread_b, spread_c, gath, lhs, part, r1, r2, r3, qsend, wg,
    upd, send2, cpart, crecv, csum, cfin,
    ld, us, ur, p1s, p1r, xs, xr, ws, wr, rs, rr, p2s, p2r, cs, cr,
):
    spread = (spread_a, spread_b, spread_c)
    g = lax.axis_index("dp")
    t = lax.axis_index("tensor")
    zl, y = g // 4, g % 4
    z, x, k = t // 8, (t // 2) % 4, t % 2
    zp = 1 - zl
    y_up, y_dn, y_far = (y + 1) % 4, (y + 3) % 4, (y + 2) % 4
    g_up, g_dn, g_pair = zl * 4 + y_up, zl * 4 + y_dn, zp * 4 + y
    x_up, x_dn = (x + 1) % 4, (x + 3) % 4
    t_xup, t_xdn = z * 8 + x_up * 2 + k, z * 8 + x_dn * 2 + k
    x_far = (x + 2) % 4
    t_core = z * 8 + x * 2 + 1 - k

    def remote(src, dst, ssem, rsem, dp, tn):
        return pltpu.make_async_remote_copy(
            src_ref=src, dst_ref=dst, send_sem=ssem, recv_sem=rsem,
            device_id=(dp, tn), device_id_type=pl.DeviceIdType.MESH,
        )

    def cols(index, width):
        return pl.ds(pl.multiple_of(index * width, width), width)

    loads = [
        pltpu.make_async_copy(src, old.at[a], ld.at[a]) for a, src in enumerate((om_ref, oo_ref, os_ref))
    ] + [pltpu.make_async_copy(tok_ref, tok, ld.at[3])]
    for c in loads:
        c.start()

    barrier = pltpu.get_barrier_semaphore()

    def greet(j, c):
        pl.semaphore_signal(barrier, inc=1, device_id=(g, (t + j) % 32), device_id_type=pl.DeviceIdType.MESH)
        return c

    lax.fori_loop(1, 32, greet, 0)
    for other in (g_up, g_dn, g_pair):
        pl.semaphore_signal(barrier, inc=1, device_id=(other, t), device_id_type=pl.DeviceIdType.MESH)

    def narrow(a):
        loads[a].wait()

        def body(i, c):
            c10, xx = i // 4, i % 4
            send1[a, c10, xx] = old[a, cols(xx, 32), cols(c10, 1024)].astype(BF)
            return c

        lax.fori_loop(0, 8, body, 0)

    narrow(0)
    pl.semaphore_wait(barrier, 34)

    def u1(dz):
        to = (z + dz) % 4
        return remote(
            up_ref.at[:, cols(to, 128)], gath.at[:, cols(x * 4 + z, 128)],
            us.at[dz], ur.at[dz], g, to * 8 + x * 2 + k,
        )

    def u1_in(dz):
        of = (z + 4 - dz) % 4
        return remote(
            up_ref.at[:, cols(z, 128)], gath.at[:, cols(x * 4 + of, 128)],
            us.at[dz], ur.at[dz], g, t_core,
        )

    u1_own = pltpu.make_async_copy(up_ref.at[:, cols(z, 128)], gath.at[:, cols(x * 4 + z, 128)], ur.at[0])
    u1_own.start()
    for dz in (2, 1, 3):
        u1(dz).start()

    def p1(a, j):
        p = (t + j) % 32
        pz, px, pk = p // 8, (p // 2) % 4, p % 2
        return remote(
            send1.at[a, :, px, :, cols(pk * 4 + pz, 128)], spread[a].at[t],
            p1s.at[a, j], p1r.at[a, j], g, p,
        )

    def p1_in(a, j):
        return remote(
            send1.at[a, :, x, :, cols(k * 4 + z, 128)], spread[a].at[(t + 32 - j) % 32],
            p1s.at[a, j], p1r.at[a, j], g, t_core,
        )

    def p1_own(a):
        return pltpu.make_async_copy(send1.at[a, :, x, :, cols(k * 4 + z, 128)], spread[a].at[t], p1r.at[a, 0])

    def p1_start(a):
        p1_own(a).start()

        def body(j, c):
            p1(a, j).start()
            return c

        lax.fori_loop(1, 32, body, 0)

    def p1_wait(a):
        p1_own(a).wait()

        def body(j, c):
            p1_in(a, j).wait_recv()
            return c

        lax.fori_loop(1, 32, body, 0)

    p1_start(0)
    narrow(1)
    narrow(2)

    loads[3].wait()
    live = cnt_ref[g]
    pick_row = lax.broadcasted_iota(jnp.int32, (128, 512), 0)
    pick_col = lax.broadcasted_iota(jnp.int32, (128, 512), 1)
    pick = jnp.where(pick_col == (pick_row // 32) * 128 + x * 32 + pick_row % 32, 1.0, 0.0).astype(BF)
    alive = lax.broadcasted_iota(jnp.int32, (128, 512), 1) < live

    def transpose_tokens(d, c):
        rows = lax.dot_general(pick, tok[:, cols(d, 512)], NT, preferred_element_type=F32)
        lhs[d % 4, cols(d // 4, 128), :] = jnp.where(alive, rows, 0.0).astype(BF)
        return c

    lax.fori_loop(0, 8, transpose_tokens, 0)

    def ring_x(block, rows, way, sem):
        ref = gath.at[rows, cols(block, 512)]
        return remote(ref, ref, xs.at[sem], xr.at[sem], g, way)

    top, bottom, whole = pl.ds(0, 256), pl.ds(256, 256), pl.ds(0, 512)
    u1_own.wait()
    for dz in (1, 2, 3):
        u1_in(dz).wait_recv()
    x_sends = [ring_x(x, whole, t_xup, 0), ring_x(x, whole, t_xdn, 1)]
    for c in x_sends:
        c.start()

    def place(q, body):
        zs, half = q % 4, q // 4
        bo, c10 = zs * 2 + half // 2, half % 2
        for so in range(4):
            body(so, bo, c10)

    def weights(q, c):
        def one(so, bo, c10):
            wg[y, pl.ds(pl.multiple_of(zl * 128 + so * 32, 32), 32), cols(q, 128)] = spread[0][inv_ref[bo * 4 + so], c10]

        place(q, one)
        return c

    def ring_w(yy, zz, to, sem):
        ref = wg.at[yy, cols(zz, 128), :]
        return remote(ref, ref, ws.at[sem], wr.at[sem], to, t)

    p1_wait(0)
    lax.fori_loop(0, 16, weights, 0)
    w_sends = [ring_w(y, zl, g_pair, 2), ring_w(y, zl, g_up, 0), ring_w(y, zl, g_dn, 1)]
    for c in w_sends:
        c.start()
    p1_start(1)
    p1_start(2)

    ring_x(x_dn, whole, t_xup, 0).wait_recv()
    x_sends.append(ring_x(x_dn, top, t_xup, 2))
    x_sends[-1].start()
    ring_x(x_up, whole, t_xdn, 1).wait_recv()
    x_sends.append(ring_x(x_up, bottom, t_xdn, 3))
    x_sends[-1].start()
    ring_x(x_far, top, t_xup, 2).wait_recv()
    ring_x(x_far, bottom, t_xdn, 3).wait_recv()

    def partial(yy):
        def body(c, carry):
            part[yy, :, cols(c, 512)] = jnp.dot(
                lhs[yy], gath[:, cols(c, 512)], preferred_element_type=F32
            ).astype(BF)
            return carry

        lax.fori_loop(0, 4, body, 0)

    def half_of(ref, yy, zz):
        return ref.at[yy, cols(zz, 128), :]

    partial(y_far)
    r_sends = [
        remote(half_of(part, y_far, 0), r1.at[0], rs.at[0], rr.at[0], g_up, t),
        remote(half_of(part, y_far, 1), r1.at[1], rs.at[1], rr.at[1], g_dn, t),
    ]
    for c in r_sends:
        c.start()
    partial(y_up)
    r_sends.append(remote(half_of(part, y_up, 1), half_of(r2, 0, 1), rs.at[2], rr.at[2], g_up, t))
    r_sends[-1].start()
    partial(y_dn)
    r_sends.append(remote(half_of(part, y_dn, 0), half_of(r2, 1, 0), rs.at[3], rr.at[3], g_dn, t))
    r_sends[-1].start()

    ring_w(y, zp, g_pair, 2).wait_recv()
    w_sends += [ring_w(y, zp, g_up, 3), ring_w(y, zp, g_dn, 4)]
    w_sends[-2].start()
    w_sends[-1].start()
    partial(y)

    def add_into(yy, zz, side):
        def body(c, carry):
            at = (yy, cols(zz, 128), cols(c, 512))
            part[at] = (part[at].astype(F32) + r1[side, :, cols(c, 512)].astype(F32)).astype(BF)
            return carry

        lax.fori_loop(0, 4, body, 0)

    r_sends[0].wait_recv()
    add_into(y_up, 0, 0)
    r_sends.append(remote(half_of(part, y_up, 0), half_of(r2, 0, 0), rs.at[4], rr.at[4], g_up, t))
    r_sends[-1].start()
    r_sends[1].wait_recv()
    add_into(y_dn, 1, 1)
    r_sends.append(remote(half_of(part, y_dn, 1), half_of(r2, 1, 1), rs.at[5], rr.at[5], g_dn, t))
    r_sends[-1].start()

    ring_w(y_dn, zl, g_up, 0).wait_recv()
    ring_w(y_dn, zp, g_up, 3).wait_recv()
    w_sends.append(ring_w(y_dn, 0, g_up, 5))
    w_sends[-1].start()
    ring_w(y_up, zl, g_dn, 1).wait_recv()
    ring_w(y_up, zp, g_dn, 4).wait_recv()
    w_sends.append(ring_w(y_up, 1, g_dn, 6))
    w_sends[-1].start()

    def back(yy):
        block = lax.dot_general(wg[yy], gath[...], NT, preferred_element_type=F32).astype(BF)
        for zz in range(2):
            for so in range(4):
                at = zz * 128 + so * 32
                cpart[zz * 4 + yy, so // 2, so % 2] = block[at : at + 32]

    back(y)
    back(y_dn)
    back(y_up)

    def sum_y(zz, c):
        at = (cols(zz, 128), cols(c, 512))
        total = part[(y, *at)].astype(F32) + r2[(0, *at)].astype(F32)
        return total + r2[(1, *at)].astype(F32)

    for s in (2, 3, 4, 5):
        r_sends[s].wait_recv()

    def for_pair(c, carry):
        qsend[:, cols(c, 512)] = sum_y(zp, c).astype(BF)
        return carry

    lax.fori_loop(0, 4, for_pair, 0)
    r_sends.append(remote(qsend, r3, rs.at[6], rr.at[6], g_pair, t))
    r_sends[-1].start()

    ring_w(y_far, 0, g_up, 5).wait_recv()
    ring_w(y_far, 1, g_dn, 6).wait_recv()
    back(y_far)
    core_send = remote(cpart.at[:, :, 1 - k], crecv, cs.at[0], cr.at[0], g, t_core)
    core_send.start()

    p1_wait(1)
    p1_wait(2)
    r_sends[6].wait_recv()
    fix_first = 1.0 - beta_first**10
    fix_second = 1.0 - beta_second**10
    scale = 1.0 / 64.0

    def step(q, carry):
        def one(so, bo, c10):
            slot = inv_ref[bo * 4 + so]
            here = cols(q, 128)
            at = pl.ds(pl.multiple_of(zl * 128 + so * 32, 32), 32)
            grad = part[y, at, here].astype(F32) + r2[0, at, here].astype(F32)
            grad = grad + r2[1, at, here].astype(F32) + r3[so * 32 : so * 32 + 32, here].astype(F32)
            grad = grad * scale
            master = spread[0][slot, c10].astype(F32)
            moment = beta_first * spread[1][slot, c10].astype(F32) + (1.0 - beta_first) * grad
            second = beta_second * spread[2][slot, c10].astype(F32) + (1.0 - beta_second) * grad * grad
            update = moment / fix_first / (jnp.sqrt(second / fix_second) + epsilon) + decay_rate * master
            piece = (bo * 2 + c10) * 2 + so // 2
            upd[piece, 0, so % 2] = (master - learn_rate * update).astype(BF)
            upd[piece, 1, so % 2] = moment.astype(BF)
            upd[piece, 2, so % 2] = second.astype(BF)

        place(q, one)
        return carry

    lax.fori_loop(0, 16, step, 0)

    def p2(j):
        p = (t + j) % 32
        return remote(
            send2.at[p], out_ref.at[:, :, x, :, cols(k * 4 + z, 128)], p2s.at[j], p2r.at[j], g, p
        )

    def p2_in(j):
        p = (t + 32 - j) % 32
        pz, px, pk = p // 8, (p // 2) % 4, p % 2
        return remote(
            send2.at[t], out_ref.at[:, :, px, :, cols(pk * 4 + pz, 128)], p2s.at[j], p2r.at[j], g, t_core
        )

    def p2_start(j, carry):
        p = (t + j) % 32
        send2[p] = upd[new_ref[p]]
        p2(j).start()
        return carry

    lax.fori_loop(1, 32, p2_start, 0)
    send2[t] = upd[new_ref[t]]
    p2_own = pltpu.make_async_copy(send2.at[t], out_ref.at[:, :, x, :, cols(k * 4 + z, 128)], p2r.at[0])
    p2_own.start()

    core_send.wait_recv()

    def add_core(d, carry):
        csum[d] = (cpart[d, :, k].astype(F32) + crecv[d].astype(F32)).astype(BF)
        return carry

    lax.fori_loop(0, 8, add_core, 0)
    me16 = z * 4 + x

    def c_out(j):
        p = (me16 + j) % 16
        return remote(csum.at[p // 2, p % 2], cfin.at[me16], cs.at[j], cr.at[j], g, p * 2 + k)

    def c_in(j):
        return remote(csum.at[0, 0], cfin.at[(me16 + 16 - j) % 16], cs.at[j], cr.at[j], g, t_core)

    core_send.wait_send()
    c_own = pltpu.make_async_copy(csum.at[me16 // 2, me16 % 2], cfin.at[me16], cr.at[0])
    c_own.start()

    def c_start(j, carry):
        c_out(j).start()
        return carry

    lax.fori_loop(1, 16, c_start, 0)
    c_own.wait()

    def c_wait(j, carry):
        c_in(j).wait_recv()
        return carry

    lax.fori_loop(1, 16, c_wait, 0)
    token = lax.broadcasted_iota(jnp.int32, (512, 128), 0)
    blocks = []
    for xx in range(4):
        total = cfin[xx].astype(F32) + cfin[4 + xx].astype(F32)
        blocks.append(total + cfin[8 + xx].astype(F32) + cfin[12 + xx].astype(F32))
    full = jnp.concatenate(blocks, axis=0) * scale
    ig_ref[...] = jnp.where(token < live, full.T, 0.0).astype(BF)

    p2_own.wait()

    def p2_wait(j, carry):
        p2_in(j).wait_recv()
        p2(j).wait_send()
        return carry

    lax.fori_loop(1, 32, p2_wait, 0)

    def c_sent(j, carry):
        c_out(j).wait_send()
        return carry

    lax.fori_loop(1, 16, c_sent, 0)

    def p1_sent(j, carry):
        for a in range(3):
            p1(a, j).wait_send()
        return carry

    lax.fori_loop(1, 32, p1_sent, 0)
    for dz in (1, 2, 3):
        u1(dz).wait_send()
    for c in x_sends + w_sends + r_sends:
        c.wait_send()


def shards(old_master, old_moment, old_second, tokens_in, upstream, counts, old_map, new_map):
    slots = jnp.arange(32, dtype=jnp.int32)
    inverse = jnp.sum(jnp.where(old_map[None, :] == slots[:, None], slots[None, :], 0), axis=1)
    hbm = pl.BlockSpec(memory_space=pl.ANY)
    smem = pl.BlockSpec(memory_space=pltpu.SMEM)
    vmem = pl.BlockSpec(memory_space=pltpu.VMEM)
    dma = pltpu.SemaphoreType.DMA
    pieces, input_grad = pl.pallas_call(
        kernel,
        out_shape=(
            jax.ShapeDtypeStruct((3, 2, 4, 32, 1024), BF),
            jax.ShapeDtypeStruct((512, 128), BF),
        ),
        in_specs=[smem] * 3 + [hbm] * 5,
        out_specs=(vmem, vmem),
        scratch_shapes=[
            pltpu.VMEM((3, 128, 2048), F32),
            pltpu.VMEM((512, 4096), BF),
            pltpu.VMEM((3, 2, 4, 32, 1024), BF),
            pltpu.VMEM((32, 2, 32, 128), BF),
            pltpu.VMEM((32, 2, 32, 128), BF),
            pltpu.VMEM((32, 2, 32, 128), BF),
            pltpu.VMEM((512, 2048), BF),
            pltpu.VMEM((4, 256, 512), BF),
            pltpu.VMEM((4, 256, 2048), BF),
            pltpu.VMEM((2, 128, 2048), BF),
            pltpu.VMEM((2, 256, 2048), BF),
            pltpu.VMEM((128, 2048), BF),
            pltpu.VMEM((128, 2048), BF),
            pltpu.VMEM((4, 256, 2048), BF),
            pltpu.VMEM((32, 3, 2, 32, 128), BF),
            pltpu.VMEM((32, 3, 2, 32, 128), BF),
            pltpu.VMEM((8, 2, 2, 32, 512), BF),
            pltpu.VMEM((8, 2, 32, 512), BF),
            pltpu.VMEM((8, 2, 32, 512), BF),
            pltpu.VMEM((16, 32, 512), BF),
            dma((4,)), dma((4,)), dma((4,)), dma((3, 32)), dma((3, 32)), dma((4,)), dma((4,)),
            dma((7,)), dma((7,)), dma((7,)), dma((7,)), dma((32,)), dma((32,)), dma((16,)), dma((16,)),
        ],
        compiler_params=pltpu.CompilerParams(
            collective_id=0, has_side_effects=True, vmem_limit_bytes=56 * 1024 * 1024
        ),
        cost_estimate=pl.CostEstimate(flops=4 * 2**30, bytes_accessed=12 * 2**20, transcendentals=2**18),
    )(
        inverse, new_map, counts,
        old_master.reshape(128, 2048), old_moment.reshape(128, 2048), old_second.reshape(128, 2048),
        tokens_in, upstream,
    )
    pieces = pieces.reshape(3, 1, 1, 256, 1024).astype(F32)
    return pieces[0], pieces[1], pieces[2], input_grad


def solution(mesh):
    pieces = P("tensor", "dp", None, None)
    return jax.shard_map(
        shards,
        mesh=mesh,
        in_specs=(pieces, pieces, pieces, P("dp", None), P("dp", "tensor"), P(), P(), P()),
        out_specs=(pieces, pieces, pieces, P("dp", "tensor")),
        check_vma=False,
    )
```

```python
import jax
import jax.numpy as jnp
from jax import lax
from jax.experimental import pallas as pl
from jax.experimental.pallas import tpu as pltpu
from jax.sharding import PartitionSpec as P

beta_first = 0.9
beta_second = 0.95
learn_rate = 0.05
decay_rate = 0.1
epsilon = 1e-08

BF = jnp.bfloat16
F32 = jnp.float32
NT = (((1,), (1,)), ((), ()))
NC = 4
PER = NC // 2
RR = 32 // PER
CT = F32


def kernel(
    inv_ref, new_ref, cnt_ref, om_ref, oo_ref, os_ref, tok_ref, up_ref,
    out_ref, ig_ref,
    old, tok, send1, spread_a, spread_b, spread_c, gath, lhs, part, r1, r2, r3, qsend, wg,
    upd, send2, cpart, crecv, csum, cfin,
    ld, us, ur, p1s, p1r, xs, xr, ws, wr, rs, rr, p2s, p2r, ks, kr, cs, cr,
):
    spread = (spread_a, spread_b, spread_c)
    g = lax.axis_index("dp")
    t = lax.axis_index("tensor")
    zl, y = g // 4, g % 4
    z, x, k = t // 8, (t // 2) % 4, t % 2
    zp = 1 - zl
    y_up, y_dn, y_far = (y + 1) % 4, (y + 3) % 4, (y + 2) % 4
    g_up, g_dn, g_pair = zl * 4 + y_up, zl * 4 + y_dn, zp * 4 + y
    x_up, x_dn, x_far = (x + 1) % 4, (x + 3) % 4, (x + 2) % 4
    t_xup, t_xdn = z * 8 + x_up * 2 + k, z * 8 + x_dn * 2 + k
    t_core = z * 8 + x * 2 + 1 - k

    def remote(src, dst, ssem, rsem, dp, tn):
        return pltpu.make_async_remote_copy(
            src_ref=src, dst_ref=dst, send_sem=ssem, recv_sem=rsem,
            device_id=(dp, tn), device_id_type=pl.DeviceIdType.MESH,
        )

    def cols(index, width):
        return pl.ds(pl.multiple_of(index * width, width), width)

    sent = []

    def start(*copies):
        for c in copies:
            c.start()
            sent.append(c)

    loads = [
        pltpu.make_async_copy(src, old.at[a], ld.at[a]) for a, src in enumerate((om_ref, oo_ref, os_ref))
    ] + [pltpu.make_async_copy(tok_ref, tok, ld.at[3])]
    for c in loads:
        c.start()

    barrier = pltpu.get_barrier_semaphore()

    def greet(j, c):
        pl.semaphore_signal(barrier, inc=1, device_id=(g, (t + j) % 32), device_id_type=pl.DeviceIdType.MESH)
        return c

    lax.fori_loop(1, 32, greet, 0)
    for other in (g_up, g_dn, g_pair):
        pl.semaphore_signal(barrier, inc=1, device_id=(other, t), device_id_type=pl.DeviceIdType.MESH)

    def narrow(a):
        loads[a].wait()

        def body(i, c):
            c10, xx = i // 4, i % 4
            send1[a, c10, xx] = old[a, cols(xx, 32), cols(c10, 1024)].astype(BF)
            return c

        lax.fori_loop(0, 8, body, 0)

    def u1(h, dz):
        to = (z + dz) % 4
        return remote(
            up_ref.at[pl.ds(h * 256, 256), cols(to, 128)], gath.at[pl.ds(h * 256, 256), cols(x * 4 + z, 128)],
            us.at[h, dz], ur.at[h, dz], g, to * 8 + x * 2 + k,
        )

    def u1_in(h, dz):
        of = (z + 4 - dz) % 4
        return remote(
            up_ref.at[pl.ds(h * 256, 256), cols(z, 128)], gath.at[pl.ds(h * 256, 256), cols(x * 4 + of, 128)],
            us.at[h, dz], ur.at[h, dz], g, t_core,
        )

    def u1_wait(h):
        if h == 0:
            u1_own.wait()
        for dz in (1, 2, 3):
            u1_in(h, dz).wait_recv()

    u1_own = pltpu.make_async_copy(up_ref.at[:, cols(z, 128)], gath.at[:, cols(x * 4 + z, 128)], ur.at[0, 0])
    def p1(a, j):
        p = (t + j) % 32
        pz, px, pk = p // 8, (p // 2) % 4, p % 2
        return remote(
            send1.at[a, :, px, :, cols(pk * 4 + pz, 128)], spread[a].at[t],
            p1s.at[a, j], p1r.at[a, j], g, p,
        )

    def p1_in(a, j):
        return remote(
            send1.at[a, :, x, :, cols(k * 4 + z, 128)], spread[a].at[(t + 32 - j) % 32],
            p1s.at[a, j], p1r.at[a, j], g, t_core,
        )

    def p1_own(a):
        return pltpu.make_async_copy(send1.at[a, :, x, :, cols(k * 4 + z, 128)], spread[a].at[t], p1r.at[a, 0])

    def p1_start(a):
        p1_own(a).start()

        def body(j, c):
            p1(a, j).start()
            return c

        lax.fori_loop(1, 32, body, 0)

    def p1_wait(a):
        p1_own(a).wait()

        def body(j, c):
            p1_in(a, j).wait_recv()
            return c

        lax.fori_loop(1, 32, body, 0)

    live = cnt_ref[g]
    pick_row = lax.broadcasted_iota(jnp.int32, (128, 512), 0)
    pick_col = lax.broadcasted_iota(jnp.int32, (128, 512), 1)
    chunk_of, so1_of = pick_row // (2 * RR), (pick_row // RR) % 2
    so_of = so1_of * 2 + chunk_of // PER
    r_of = (chunk_of % PER) * RR + pick_row % RR
    pick = jnp.where(pick_col == so_of * 128 + x * 32 + r_of, 1.0, 0.0).astype(BF)
    alive = lax.broadcasted_iota(jnp.int32, (128, 512), 1) < live

    def transpose_tokens(d, c):
        rows = lax.dot_general(pick, tok[:, cols(d, 512)], NT, preferred_element_type=F32)
        rows = jnp.where(alive, rows, 0.0).astype(BF)
        for i in range(NC):
            lhs[i, cols((d % 4) * 2 + d // 4, 2 * RR), :] = rows[i * 2 * RR : (i + 1) * 2 * RR]
        return c

    def ring_x(block, h, way, sem):
        ref = gath.at[pl.ds(h * 256, 256), cols(block, 512)]
        return remote(ref, ref, xs.at[sem], xr.at[sem], g, way)

    def place(q):
        zs, half = q % 4, q // 4
        return zs * 2 + half // 2, half % 2

    def weights(q, c):
        bo, c10 = place(q)
        for so in range(4):
            wg[y, pl.ds(pl.multiple_of(zl * 128 + so * 32, 32), 32), cols(q, 128)] = spread[0][inv_ref[bo * 4 + so], c10]
        return c

    def ring_w(yy, zz, to, sem):
        ref = wg.at[yy, cols(zz, 128), :]
        return remote(ref, ref, ws.at[sem], wr.at[sem], to, t)

    def block(ref, i, yy, zz):
        return ref.at[i, cols(yy * 2 + zz, 2 * RR), :]

    def partial(i):
        def body(c, carry):
            part[i, :, cols(c, 512)] = jnp.dot(
                lhs[i], gath[:, cols(c, 512)], preferred_element_type=F32
            ).astype(BF)
            return carry

        lax.fori_loop(0, 4, body, 0)

    def sum_copy(i, n, src, dst, to):
        return remote(src, dst, rs.at[i, n], rr.at[i, n], to, t)

    def far_up(i):
        return sum_copy(i, 0, block(part, i, y_far, 0), r1.at[i, 0], g_up)

    def far_dn(i):
        return sum_copy(i, 1, block(part, i, y_far, 1), r1.at[i, 1], g_dn)

    def near_up(i, zz):
        return sum_copy(i, 2 + zz, block(part, i, y_up, zz), r2.at[i, 0, zz], g_up)

    def near_dn(i, zz):
        return sum_copy(i, 4 + zz, block(part, i, y_dn, zz), r2.at[i, 1, zz], g_dn)

    def pair_copy(i):
        return sum_copy(i, 6, qsend.at[i], r3.at[i], g_pair)

    def add_into(i, yy, zz, side):
        def body(c, carry):
            at = (i, cols(yy * 2 + zz, 2 * RR), cols(c, 512))
            part[at] = (part[at].astype(F32) + r1[i, side, :, cols(c, 512)].astype(F32)).astype(BF)
            return carry

        lax.fori_loop(0, 4, body, 0)

    def sum_first(i):
        start(far_up(i), far_dn(i), near_up(i, 1), near_dn(i, 0))

    def sum_second(i):
        far_up(i).wait_recv()
        add_into(i, y_up, 0, 0)
        start(near_up(i, 0))
        far_dn(i).wait_recv()
        add_into(i, y_dn, 1, 1)
        start(near_dn(i, 1))

    def sum_third(i):
        for zz in range(2):
            near_up(i, zz).wait_recv()
            near_dn(i, zz).wait_recv()

        def body(c, carry):
            here = cols(c, 512)
            total = part[i, cols(y * 2 + zp, 2 * RR), here].astype(F32) + r2[i, 0, zp, :, here].astype(F32)
            qsend[i, :, here] = (total + r2[i, 1, zp, :, here].astype(F32)).astype(BF)
            return carry

        lax.fori_loop(0, 4, body, 0)
        start(pair_copy(i))

    fix_first = 1.0 - beta_first**10
    fix_second = 1.0 - beta_second**10
    scale = 1.0 / 64.0

    def adamw(i):
        pair_copy(i).wait_recv()
        so0, r0 = i // PER, (i % PER) * RR

        def body(q, carry):
            bo, c10 = place(q)
            here = cols(q, 128)
            for so1 in range(2):
                slot = inv_ref[bo * 4 + so1 * 2 + so0]
                at = slice(so1 * RR, (so1 + 1) * RR)
                mine = pl.ds(pl.multiple_of((y * 2 + zl) * 2 * RR + so1 * RR, RR), RR)
                grad = part[i, mine, here].astype(F32) + r2[i, 0, zl, at, here].astype(F32)
                grad = grad + r2[i, 1, zl, at, here].astype(F32) + r3[i, at, here].astype(F32)
                grad = grad * scale
                rows = slice(r0, r0 + RR)
                master = spread[0][slot, c10, rows].astype(F32)
                moment = beta_first * spread[1][slot, c10, rows].astype(F32) + (1.0 - beta_first) * grad
                second = beta_second * spread[2][slot, c10, rows].astype(F32) + (1.0 - beta_second) * grad * grad
                update = moment / fix_first / (jnp.sqrt(second / fix_second) + epsilon) + decay_rate * master
                piece = (bo * 2 + c10) * 2 + so1
                upd[i, piece, 0] = (master - learn_rate * update).astype(BF)
                upd[i, piece, 1] = moment.astype(BF)
                upd[i, piece, 2] = second.astype(BF)
            return carry

        lax.fori_loop(0, 16, body, 0)

    def p2_place(i, px, pk, pz):
        return out_ref.at[:, i // PER, px, pl.ds((i % PER) * RR, RR), cols(pk * 4 + pz, 128)]

    def p2(i, j):
        p = (t + j) % 32
        return remote(send2[i].at[p], p2_place(i, x, k, z), p2s.at[i, j], p2r.at[i, j], g, p)

    def p2_in(i, j):
        p = (t + 32 - j) % 32
        return remote(
            send2[i].at[t], p2_place(i, (p // 2) % 4, p % 2, p // 8), p2s.at[i, j], p2r.at[i, j], g, t_core
        )

    def p2_own(i):
        return pltpu.make_async_copy(send2[i].at[t], p2_place(i, x, k, z), p2r.at[i, 0])

    def p2_start(i):
        def body(j, carry):
            p = (t + j) % 32
            send2[i][p] = upd[i, new_ref[p]]
            p2(i, j).start()
            return carry

        lax.fori_loop(1, 32, body, 0)
        send2[i][t] = upd[i, new_ref[t]]
        p2_own(i).start()

    def back(yy):
        rows = lax.dot_general(wg[yy], gath[...], NT, preferred_element_type=F32)
        for zz in range(2):
            for so in range(4):
                at = zz * 128 + so * 32
                cpart[zz * 4 + yy, so // 2, so % 2] = rows[at : at + 32].astype(CT)

    def core_copy(i, yy, zz):
        return remote(
            cpart.at[zz * 4 + yy, :, 1 - k], crecv.at[zz * 4 + yy], ks.at[i, zz], kr.at[i, zz], g, t_core
        )

    def back_send(i, yy):
        back(yy)
        start(core_copy(i, yy, 0), core_copy(i, yy, 1))

    me16 = z * 4 + x

    def c_out(p):
        j = (p - me16 + 16) % 16
        return remote(csum.at[p // 2, p % 2], cfin.at[me16], cs.at[j], cr.at[j], g, p * 2 + k)

    c_own = pltpu.make_async_copy(csum.at[me16 // 2, me16 % 2], cfin.at[me16], cr.at[0])

    def back_sum(i, yy):
        for zz in range(2):
            d = zz * 4 + yy
            core_copy(i, yy, zz).wait_recv()
            csum[d] = (cpart[d, :, k].astype(F32) + crecv[d].astype(F32)).astype(BF)
            for so1 in range(2):
                p = d * 2 + so1

                @pl.when(p != me16)
                def _():
                    c_out(p).start()

                @pl.when(p == me16)
                def _():
                    c_own.start()

    pl.semaphore_wait(barrier, 34)
    u1_own.start()
    narrow(0)
    p1_start(0)
    loads[3].wait()
    lax.fori_loop(0, 8, transpose_tokens, 0)
    for h in range(2):
        for dz in (2, 1, 3):
            start(u1(h, dz))
    narrow(1)
    narrow(2)
    p1_wait(0)
    lax.fori_loop(0, 16, weights, 0)
    start(ring_w(y, zl, g_pair, 2), ring_w(y, zl, g_up, 0), ring_w(y, zl, g_dn, 1))
    u1_wait(0)
    start(ring_x(x, 0, t_xup, 0))
    u1_wait(1)
    start(ring_x(x, 1, t_xdn, 1), ring_x(x, 1, t_xup, 2), ring_x(x, 0, t_xdn, 3))
    p1_start(1)
    p1_start(2)
    ring_w(y_dn, zl, g_up, 0).wait_recv()
    start(ring_w(y_dn, zl, g_up, 5))
    ring_w(y_up, zl, g_dn, 1).wait_recv()
    ring_w(y, zp, g_pair, 2).wait_recv()
    start(ring_w(y, zp, g_up, 3), ring_w(y, zp, g_dn, 4))
    ring_x(x_dn, 0, t_xup, 0).wait_recv()
    start(ring_x(x_dn, 0, t_xup, 4))
    ring_x(x_up, 1, t_xdn, 1).wait_recv()
    start(ring_x(x_up, 1, t_xdn, 5))
    ring_x(x_dn, 1, t_xup, 2).wait_recv()
    ring_x(x_up, 0, t_xdn, 3).wait_recv()
    ring_x(x_far, 0, t_xup, 4).wait_recv()
    ring_x(x_far, 1, t_xdn, 5).wait_recv()
    partial(0)
    sum_first(0)
    ring_w(y_up, zp, g_dn, 4).wait_recv()
    start(ring_w(y_up, zp, g_dn, 6))
    back_send(0, y)
    partial(1)
    sum_first(1)
    sum_second(0)
    partial(2)
    sum_first(2)
    ring_w(y_dn, zp, g_up, 3).wait_recv()
    back_send(1, y_dn)
    back_send(2, y_up)
    back_sum(0, y)
    sum_second(1)
    sum_third(0)
    back_sum(1, y_dn)
    back_sum(2, y_up)
    partial(3)
    sum_first(3)
    ring_w(y_far, zl, g_up, 5).wait_recv()
    ring_w(y_far, zp, g_dn, 6).wait_recv()
    back_send(3, y_far)
    sum_second(2)
    sum_third(1)
    p1_wait(1)
    p1_wait(2)
    back_sum(3, y_far)
    adamw(0)
    p2_start(0)
    sum_second(3)
    sum_third(2)
    adamw(1)
    p2_start(1)
    sum_third(3)
    adamw(2)
    p2_start(2)
    adamw(3)
    p2_start(3)

    c_own.wait()

    def c_wait(j, carry):
        remote(csum.at[0, 0], cfin.at[(me16 + 16 - j) % 16], cs.at[j], cr.at[j], g, t_core).wait_recv()
        return carry

    lax.fori_loop(1, 16, c_wait, 0)
    token = lax.broadcasted_iota(jnp.int32, (512, 128), 0)
    blocks = []
    for xx in range(4):
        total = cfin[xx].astype(F32) + cfin[4 + xx].astype(F32)
        blocks.append(total + cfin[8 + xx].astype(F32) + cfin[12 + xx].astype(F32))
    full = jnp.concatenate(blocks, axis=0) * scale
    ig_ref[...] = jnp.where(token < live, full.T, 0.0).astype(BF)

    for i in range(NC):
        p2_own(i).wait()

        def p2_wait(j, carry):
            p2_in(i, j).wait_recv()
            p2(i, j).wait_send()
            return carry

        lax.fori_loop(1, 32, p2_wait, 0)

    def c_sent(j, carry):
        c_out((me16 + j) % 16).wait_send()
        return carry

    lax.fori_loop(1, 16, c_sent, 0)

    def p1_sent(j, carry):
        for a in range(3):
            p1(a, j).wait_send()
        return carry

    lax.fori_loop(1, 32, p1_sent, 0)
    for c in sent:
        c.wait_send()


def shards(old_master, old_moment, old_second, tokens_in, upstream, counts, old_map, new_map):
    slots = jnp.arange(32, dtype=jnp.int32)
    inverse = jnp.sum(jnp.where(old_map[None, :] == slots[:, None], slots[None, :], 0), axis=1)
    hbm = pl.BlockSpec(memory_space=pl.ANY)
    smem = pl.BlockSpec(memory_space=pltpu.SMEM)
    vmem = pl.BlockSpec(memory_space=pltpu.VMEM)
    dma = pltpu.SemaphoreType.DMA
    pieces, input_grad = pl.pallas_call(
        kernel,
        out_shape=(
            jax.ShapeDtypeStruct((3, 2, 4, 32, 1024), BF),
            jax.ShapeDtypeStruct((512, 128), BF),
        ),
        in_specs=[smem] * 3 + [hbm] * 5,
        out_specs=(vmem, vmem),
        scratch_shapes=[
            pltpu.VMEM((3, 128, 2048), F32),
            pltpu.VMEM((512, 4096), BF),
            pltpu.VMEM((3, 2, 4, 32, 1024), BF),
            pltpu.VMEM((32, 2, 32, 128), BF),
            pltpu.VMEM((32, 2, 32, 128), BF),
            pltpu.VMEM((32, 2, 32, 128), BF),
            pltpu.VMEM((512, 2048), BF),
            pltpu.VMEM((NC, 16 * RR, 512), BF),
            pltpu.VMEM((NC, 16 * RR, 2048), BF),
            pltpu.VMEM((NC, 2, 2 * RR, 2048), BF),
            pltpu.VMEM((NC, 2, 2, 2 * RR, 2048), BF),
            pltpu.VMEM((NC, 2 * RR, 2048), BF),
            pltpu.VMEM((NC, 2 * RR, 2048), BF),
            pltpu.VMEM((4, 256, 2048), BF),
            pltpu.VMEM((NC, 32, 3, RR, 128), BF),
            [pltpu.VMEM((32, 3, RR, 128), BF)] * NC,
            pltpu.VMEM((8, 2, 2, 32, 512), CT),
            pltpu.VMEM((8, 2, 32, 512), CT),
            pltpu.VMEM((8, 2, 32, 512), BF),
            pltpu.VMEM((16, 32, 512), BF),
            dma((4,)), dma((2, 4)), dma((2, 4)), dma((3, 32)), dma((3, 32)), dma((6,)), dma((6,)),
            dma((7,)), dma((7,)), dma((NC, 7)), dma((NC, 7)), dma((NC, 32)), dma((NC, 32)),
            dma((4, 2)), dma((4, 2)), dma((16,)), dma((16,)),
        ],
        compiler_params=pltpu.CompilerParams(
            collective_id=0, has_side_effects=True, vmem_limit_bytes=56 * 1024 * 1024
        ),
        cost_estimate=pl.CostEstimate(flops=4 * 2**30, bytes_accessed=12 * 2**20, transcendentals=2**18),
    )(
        inverse, new_map, counts,
        old_master.reshape(128, 2048), old_moment.reshape(128, 2048), old_second.reshape(128, 2048),
        tokens_in, upstream,
    )
    pieces = pieces.reshape(3, 1, 1, 256, 1024).astype(F32)
    return pieces[0], pieces[1], pieces[2], input_grad


def solution(mesh):
    pieces = P("tensor", "dp", None, None)
    return jax.shard_map(
        shards,
        mesh=mesh,
        in_specs=(pieces, pieces, pieces, P("dp", None), P("dp", "tensor"), P(), P(), P()),
        out_specs=(pieces, pieces, pieces, P("dp", "tensor")),
        check_vma=False,
    )
```

```python
import jax
import jax.numpy as jnp
from jax import lax
from jax.experimental import pallas as pl
from jax.experimental.pallas import tpu as pltpu
from jax.sharding import PartitionSpec as P

beta_first = 0.9
beta_second = 0.95
learn_rate = 0.05
decay_rate = 0.1
epsilon = 1e-08

BF = jnp.bfloat16
F32 = jnp.float32
NT = (((1,), (1,)), ((), ()))
NC = 4
PER = NC // 2
RR = 32 // PER
CT = F32


def kernel(
    inv_ref, new_ref, cnt_ref, om_ref, oo_ref, os_ref, tok_ref, up_ref,
    out_ref, ig_ref,
    old, tok, send1, spread_a, spread_b, spread_c, gath, lhs, tsend, acc, part, r1, r2, wg,
    upd, send2, cpart, crecv, csum, cfin,
    ld, us, ur, es, er, ts, tr, p1s, p1r, xs, xr, ws, wr, rs, rr, p2s, p2r, ks, kr, cs, cr,
):
    spread = (spread_a, spread_b, spread_c)
    g = lax.axis_index("dp")
    t = lax.axis_index("tensor")
    zl, y = g // 4, g % 4
    z, x, k = t // 8, (t // 2) % 4, t % 2
    zp = 1 - zl
    y_up, y_dn, y_far = (y + 1) % 4, (y + 3) % 4, (y + 2) % 4
    g_up, g_dn, g_pair = zl * 4 + y_up, zl * 4 + y_dn, zp * 4 + y
    x_up, x_dn, x_far = (x + 1) % 4, (x + 3) % 4, (x + 2) % 4
    t_xup, t_xdn = z * 8 + x_up * 2 + k, z * 8 + x_dn * 2 + k
    t_core = z * 8 + x * 2 + 1 - k

    def remote(src, dst, ssem, rsem, dp, tn):
        return pltpu.make_async_remote_copy(
            src_ref=src, dst_ref=dst, send_sem=ssem, recv_sem=rsem,
            device_id=(dp, tn), device_id_type=pl.DeviceIdType.MESH,
        )

    def cols(index, width):
        return pl.ds(pl.multiple_of(index * width, width), width)

    sent = []

    def start(*copies):
        for c in copies:
            c.start()
            sent.append(c)

    loads = [
        pltpu.make_async_copy(src, old.at[a], ld.at[a]) for a, src in enumerate((om_ref, oo_ref, os_ref))
    ] + [pltpu.make_async_copy(tok_ref, tok, ld.at[3])]
    for c in loads:
        c.start()

    barrier = pltpu.get_barrier_semaphore()

    def greet(j, c):
        pl.semaphore_signal(barrier, inc=1, device_id=(g, (t + j) % 32), device_id_type=pl.DeviceIdType.MESH)
        return c

    lax.fori_loop(1, 32, greet, 0)
    for other in (g_up, g_dn):
        pl.semaphore_signal(barrier, inc=1, device_id=(other, t), device_id_type=pl.DeviceIdType.MESH)

    def greet_pair(j, c):
        pl.semaphore_signal(barrier, inc=1, device_id=(g_pair, j * 2 + k), device_id_type=pl.DeviceIdType.MESH)
        return c

    lax.fori_loop(0, 16, greet_pair, 0)

    def narrow(a):
        loads[a].wait()

        def body(i, c):
            c10, xx = i // 4, i % 4
            send1[a, c10, xx] = old[a, cols(xx, 32), cols(c10, 1024)].astype(BF)
            return c

        lax.fori_loop(0, 8, body, 0)

    def half(zz, h):
        return pl.ds(pl.multiple_of(zz * 512 + h * 256, 256), 256)

    def u1(h, dz):
        to = (z + dz) % 4
        return remote(
            up_ref.at[pl.ds(h * 256, 256), cols(to, 128)], gath.at[half(zl, h), cols(x * 4 + z, 128)],
            us.at[h, dz], ur.at[h, dz], g, to * 8 + x * 2 + k,
        )

    def u1_in(h, dz):
        of = (z + 4 - dz) % 4
        return remote(
            up_ref.at[pl.ds(h * 256, 256), cols(z, 128)], gath.at[half(zl, h), cols(x * 4 + of, 128)],
            us.at[h, dz], ur.at[h, dz], g, t_core,
        )

    def u1_wait(h):
        if h == 0:
            u1_own.wait()
        for dz in (1, 2, 3):
            u1_in(h, dz).wait_recv()

    u1_own = pltpu.make_async_copy(up_ref.at[:, cols(z, 128)], gath.at[cols(zl, 512), cols(x * 4 + z, 128)], ur.at[0, 0])

    def u2(zz, h):
        ref = gath.at[half(zz, h), cols(x, 512)]
        return remote(ref, ref, es.at[h], er.at[h], g_pair, t)

    def p1(a, j):
        p = (t + j) % 32
        pz, px, pk = p // 8, (p // 2) % 4, p % 2
        return remote(
            send1.at[a, :, px, :, cols(pk * 4 + pz, 128)], spread[a].at[t],
            p1s.at[a, j], p1r.at[a, j], g, p,
        )

    def p1_in(a, j):
        return remote(
            send1.at[a, :, x, :, cols(k * 4 + z, 128)], spread[a].at[(t + 32 - j) % 32],
            p1s.at[a, j], p1r.at[a, j], g, t_core,
        )

    def p1_own(a):
        return pltpu.make_async_copy(send1.at[a, :, x, :, cols(k * 4 + z, 128)], spread[a].at[t], p1r.at[a, 0])

    def p1_start(a):
        p1_own(a).start()

        def body(j, c):
            p1(a, j).start()
            return c

        lax.fori_loop(1, 32, body, 0)

    def p1_wait(a):
        p1_own(a).wait()

        def body(j, c):
            p1_in(a, j).wait_recv()
            return c

        lax.fori_loop(1, 32, body, 0)

    live = cnt_ref[g]
    pick_row = lax.broadcasted_iota(jnp.int32, (128, 512), 0)
    pick_col = lax.broadcasted_iota(jnp.int32, (128, 512), 1)
    chunk_of, so1_of = pick_row // (2 * RR), (pick_row // RR) % 2
    so_of = so1_of * 2 + chunk_of // PER
    r_of = (chunk_of % PER) * RR + pick_row % RR
    pick = jnp.where(pick_col == so_of * 128 + x * 32 + r_of, 1.0, 0.0).astype(BF)
    alive = lax.broadcasted_iota(jnp.int32, (128, 512), 1) < live

    def transpose_tokens(yy, c):
        for zz, ref, where in ((zl, lhs, cols(zl, 512)), (zp, tsend, pl.ds(0, 512))):
            rows = lax.dot_general(pick, tok[:, cols(zz * 4 + yy, 512)], NT, preferred_element_type=F32)
            rows = jnp.where(alive, rows, 0.0).astype(BF)
            for i in range(NC):
                ref[cols(i * 4 + yy, 2 * RR), where] = rows[i * 2 * RR : (i + 1) * 2 * RR]
        return c

    def tokens_pair(zz, kk):
        rows = cols(kk, 256)
        return remote(tsend.at[rows], lhs.at[rows, cols(zz, 512)], ts.at[0], tr.at[0], g_pair, t)

    def tokens_core(kk):
        ref = lhs.at[cols(kk, 256), cols(zp, 512)]
        return remote(ref, ref, ts.at[1], tr.at[1], g, t_core)

    def ring_x(zz, block, h, way, sem):
        ref = gath.at[half(zz, h), cols(block, 512)]
        at = sem if zz is zl else 6 + sem
        return remote(ref, ref, xs.at[at], xr.at[at], g, way)

    def place(q):
        zs, half = q % 4, q // 4
        return zs * 2 + half // 2, half % 2

    def weights(q, c):
        bo, c10 = place(q)
        for so in range(4):
            wg[cols(y * 4 + so, 32), cols(q, 128)] = spread[0][inv_ref[bo * 4 + so], c10]
        return c

    def ring_w(yy, start_row, rows, to, sem):
        ref = wg.at[pl.ds(pl.multiple_of(yy * 128 + start_row, 64), rows), :]
        return remote(ref, ref, ws.at[sem], wr.at[sem], to, t)

    def block(i, yy, so1):
        return part.at[cols(i * 8 + yy * 2 + so1, RR), :]

    def partial(zz):
        def body(c, carry):
            here = cols(c, 512)
            product = jnp.dot(
                lhs[:, cols(zz, 512)], gath[cols(zz, 512), here], preferred_element_type=F32
            )
            if zz is zl:
                acc[:, here] = product
            else:
                part[:, here] = (acc[:, here] + product).astype(BF)
            return carry

        lax.fori_loop(0, 4, body, 0)

    def sum_copy(i, n, src, dst, to):
        return remote(src, dst, rs.at[i, n], rr.at[i, n], to, t)

    def far_up(i):
        return sum_copy(i, 0, block(i, y_far, 0), r1.at[i, 0], g_up)

    def far_dn(i):
        return sum_copy(i, 1, block(i, y_far, 1), r1.at[i, 1], g_dn)

    def near_up(i, so1):
        return sum_copy(i, 2 + so1, block(i, y_up, so1), r2.at[i, 0, so1], g_up)

    def near_dn(i, so1):
        return sum_copy(i, 4 + so1, block(i, y_dn, so1), r2.at[i, 1, so1], g_dn)

    def add_into(i, yy, so1):
        def body(c, carry):
            at = (cols(i * 8 + yy * 2 + so1, RR), cols(c, 512))
            part[at] = (part[at].astype(F32) + r1[i, so1, :, cols(c, 512)].astype(F32)).astype(BF)
            return carry

        lax.fori_loop(0, 4, body, 0)

    def sum_first(i):
        start(far_up(i), far_dn(i), near_up(i, 1), near_dn(i, 0))

    def sum_second(i):
        far_up(i).wait_recv()
        add_into(i, y_up, 0)
        start(near_up(i, 0))
        far_dn(i).wait_recv()
        add_into(i, y_dn, 1)
        start(near_dn(i, 1))

    fix_first = 1.0 - beta_first**10
    fix_second = 1.0 - beta_second**10
    scale = 1.0 / 64.0

    def adamw(i):
        for so1 in range(2):
            near_up(i, so1).wait_recv()
            near_dn(i, so1).wait_recv()
        so0, r0 = i // PER, (i % PER) * RR

        def body(q, carry):
            bo, c10 = place(q)
            here = cols(q, 128)
            for so1 in range(2):
                slot = inv_ref[bo * 4 + so1 * 2 + so0]
                mine = cols(i * 8 + y * 2 + so1, RR)
                grad = part[mine, here].astype(F32) + r2[i, 0, so1, :, here].astype(F32)
                grad = grad + r2[i, 1, so1, :, here].astype(F32)
                grad = grad * scale
                rows = slice(r0, r0 + RR)
                master = spread[0][slot, c10, rows].astype(F32)
                moment = beta_first * spread[1][slot, c10, rows].astype(F32) + (1.0 - beta_first) * grad
                second = beta_second * spread[2][slot, c10, rows].astype(F32) + (1.0 - beta_second) * grad * grad
                update = moment / fix_first / (jnp.sqrt(second / fix_second) + epsilon) + decay_rate * master
                piece = (bo * 2 + c10) * 2 + so1
                upd[i, piece, 0] = (master - learn_rate * update).astype(BF)
                upd[i, piece, 1] = moment.astype(BF)
                upd[i, piece, 2] = second.astype(BF)
            return carry

        lax.fori_loop(0, 16, body, 0)

    def p2_place(i, px, pk, pz):
        return out_ref.at[:, i // PER, px, pl.ds((i % PER) * RR, RR), cols(pk * 4 + pz, 128)]

    def p2(i, j):
        p = (t + j) % 32
        return remote(send2[i].at[p], p2_place(i, x, k, z), p2s.at[i, j], p2r.at[i, j], g, p)

    def p2_in(i, j):
        p = (t + 32 - j) % 32
        return remote(
            send2[i].at[t], p2_place(i, (p // 2) % 4, p % 2, p // 8), p2s.at[i, j], p2r.at[i, j], g, t_core
        )

    def p2_own(i):
        return pltpu.make_async_copy(send2[i].at[t], p2_place(i, x, k, z), p2r.at[i, 0])

    def p2_start(i):
        def body(j, carry):
            p = (t + j) % 32
            send2[i][p] = upd[i, new_ref[p]]
            p2(i, j).start()
            return carry

        lax.fori_loop(1, 32, body, 0)
        send2[i][t] = upd[i, new_ref[t]]
        p2_own(i).start()

    def back(tz):
        def body(c, carry):
            rows = lax.dot_general(
                wg[...], gath[cols(tz * 2 + c, 256), :], NT, preferred_element_type=F32
            )
            for yy in range(4):
                for so in range(4):
                    at = yy * 128 + so * 32
                    cpart[tz, yy, so // 2, so % 2, :, cols(c, 256)] = rows[at : at + 32].astype(CT)
            return carry

        lax.fori_loop(0, 2, body, 0)

    def core_copy(tz):
        at = 0 if tz is zl else 1
        return remote(cpart.at[tz, :, :, 1 - k], crecv.at[tz], ks.at[at], kr.at[at], g, t_core)

    def back_send(tz):
        back(tz)
        start(core_copy(tz))

    me16 = z * 4 + x
    c_own = pltpu.make_async_copy(csum.at[zl, (z % 2) * 2 + x // 2, x % 2], cfin.at[me16], cr.at[me16])

    def c_parts(tz):
        for yy in range(4):
            for so1 in range(2):
                pz, px = zl * 2 + yy // 2, (yy % 2) * 2 + so1
                here = jnp.logical_and(pz == z, px == x)
                copy = remote(
                    csum.at[tz, yy, so1], cfin.at[me16], cs.at[0 if tz is zl else 1, yy, so1], cr.at[me16],
                    tz * 4 + y, pz * 8 + px * 2 + k,
                )
                yield here, copy

    def back_sum(tz):
        core_copy(tz).wait_recv()

        def body(yy, carry):
            csum[tz, yy] = (cpart[tz, yy, :, k].astype(F32) + crecv[tz, yy].astype(F32)).astype(BF)
            return carry

        lax.fori_loop(0, 4, body, 0)
        for here, copy in c_parts(tz):
            if tz is zl:

                @pl.when(jnp.logical_not(here))
                def _():
                    copy.start()

                @pl.when(here)
                def _():
                    c_own.start()

            else:
                start(copy)

    narrow(0)
    pl.semaphore_wait(barrier, 49)
    u1_own.start()
    for h in range(2):
        for dz in (2, 1, 3):
            start(u1(h, dz))
    loads[3].wait()
    lax.fori_loop(0, 4, transpose_tokens, 0)
    narrow(1)
    narrow(2)
    u1_wait(0)
    start(ring_x(zl, x, 0, t_xup, 0), u2(zl, 0))
    p1_start(0)
    u1_wait(1)
    start(ring_x(zl, x, 1, t_xdn, 1), u2(zl, 1), ring_x(zl, x, 1, t_xup, 2), ring_x(zl, x, 0, t_xdn, 3))
    start(tokens_pair(zl, k))
    ring_x(zl, x_dn, 0, t_xup, 0).wait_recv()
    start(ring_x(zl, x_dn, 0, t_xup, 4))
    ring_x(zl, x_up, 1, t_xdn, 1).wait_recv()
    start(ring_x(zl, x_up, 1, t_xdn, 5))
    u2(zp, 0).wait_recv()
    start(ring_x(zp, x, 0, t_xup, 0))
    u2(zp, 1).wait_recv()
    start(ring_x(zp, x, 1, t_xdn, 1), ring_x(zp, x, 1, t_xup, 2), ring_x(zp, x, 0, t_xdn, 3))
    p1_start(1)
    p1_wait(0)
    lax.fori_loop(0, 16, weights, 0)
    start(ring_w(y, 0, 128, g_up, 0), ring_w(y, 0, 128, g_dn, 1))
    p1_start(2)
    tokens_pair(zp, k).wait_recv()
    start(tokens_core(k))
    ring_x(zp, x_dn, 0, t_xup, 0).wait_recv()
    start(ring_x(zp, x_dn, 0, t_xup, 4))
    ring_x(zp, x_up, 1, t_xdn, 1).wait_recv()
    start(ring_x(zp, x_up, 1, t_xdn, 5))
    ring_w(y_dn, 0, 128, g_up, 0).wait_recv()
    start(ring_w(y_dn, 0, 64, g_up, 2))
    ring_w(y_up, 0, 128, g_dn, 1).wait_recv()
    start(ring_w(y_up, 64, 64, g_dn, 3))
    ring_x(zl, x_dn, 1, t_xup, 2).wait_recv()
    ring_x(zl, x_up, 0, t_xdn, 3).wait_recv()
    ring_x(zl, x_far, 0, t_xup, 4).wait_recv()
    ring_x(zl, x_far, 1, t_xdn, 5).wait_recv()
    partial(zl)
    ring_w(y_far, 0, 64, g_up, 2).wait_recv()
    ring_w(y_far, 64, 64, g_dn, 3).wait_recv()
    back_send(zl)
    back_sum(zl)
    ring_x(zp, x_dn, 1, t_xup, 2).wait_recv()
    ring_x(zp, x_up, 0, t_xdn, 3).wait_recv()
    ring_x(zp, x_far, 0, t_xup, 4).wait_recv()
    ring_x(zp, x_far, 1, t_xdn, 5).wait_recv()
    tokens_core(1 - k).wait_recv()
    partial(zp)
    sum_first(0)
    sum_first(1)
    back_send(zp)
    sum_second(0)
    sum_first(2)
    sum_second(1)
    sum_first(3)
    p1_wait(1)
    p1_wait(2)
    adamw(0)
    p2_start(0)
    back_sum(zp)
    sum_second(2)
    adamw(1)
    p2_start(1)
    sum_second(3)
    adamw(2)
    p2_start(2)
    adamw(3)
    p2_start(3)

    def c_wait(j, carry):
        remote(csum.at[0, 0, 0], cfin.at[j], cs.at[0, 0, 0], cr.at[j], g, t_core).wait_recv()
        return carry

    lax.fori_loop(0, 16, c_wait, 0)
    token = lax.broadcasted_iota(jnp.int32, (512, 128), 0)
    blocks = []
    for xx in range(4):
        total = cfin[xx].astype(F32) + cfin[4 + xx].astype(F32)
        blocks.append(total + cfin[8 + xx].astype(F32) + cfin[12 + xx].astype(F32))
    full = jnp.concatenate(blocks, axis=0) * scale
    ig_ref[...] = jnp.where(token < live, full.T, 0.0).astype(BF)

    for i in range(NC):
        p2_own(i).wait()

        def p2_wait(j, carry):
            p2_in(i, j).wait_recv()
            p2(i, j).wait_send()
            return carry

        lax.fori_loop(1, 32, p2_wait, 0)

    for here, copy in c_parts(zl):

        @pl.when(jnp.logical_not(here))
        def _():
            copy.wait_send()


    def p1_sent(j, carry):
        for a in range(3):
            p1(a, j).wait_send()
        return carry

    lax.fori_loop(1, 32, p1_sent, 0)
    for c in sent:
        c.wait_send()


def shards(old_master, old_moment, old_second, tokens_in, upstream, counts, old_map, new_map):
    slots = jnp.arange(32, dtype=jnp.int32)
    inverse = jnp.sum(jnp.where(old_map[None, :] == slots[:, None], slots[None, :], 0), axis=1)
    hbm = pl.BlockSpec(memory_space=pl.ANY)
    smem = pl.BlockSpec(memory_space=pltpu.SMEM)
    vmem = pl.BlockSpec(memory_space=pltpu.VMEM)
    dma = pltpu.SemaphoreType.DMA
    pieces, input_grad = pl.pallas_call(
        kernel,
        out_shape=(
            jax.ShapeDtypeStruct((3, 2, 4, 32, 1024), BF),
            jax.ShapeDtypeStruct((512, 128), BF),
        ),
        in_specs=[smem] * 3 + [hbm] * 5,
        out_specs=(vmem, vmem),
        scratch_shapes=[
            pltpu.VMEM((3, 128, 2048), F32),
            pltpu.VMEM((512, 4096), BF),
            pltpu.VMEM((3, 2, 4, 32, 1024), BF),
            pltpu.VMEM((32, 2, 32, 128), BF),
            pltpu.VMEM((32, 2, 32, 128), BF),
            pltpu.VMEM((32, 2, 32, 128), BF),
            pltpu.VMEM((1024, 2048), BF),
            pltpu.VMEM((512, 1024), BF),
            pltpu.VMEM((512, 512), BF),
            pltpu.VMEM((512, 2048), F32),
            pltpu.VMEM((512, 2048), BF),
            pltpu.VMEM((NC, 2, RR, 2048), BF),
            pltpu.VMEM((NC, 2, 2, RR, 2048), BF),
            pltpu.VMEM((512, 2048), BF),
            pltpu.VMEM((NC, 32, 3, RR, 128), BF),
            [pltpu.VMEM((32, 3, RR, 128), BF)] * NC,
            pltpu.VMEM((2, 4, 2, 2, 32, 512), CT),
            pltpu.VMEM((2, 4, 2, 32, 512), CT),
            pltpu.VMEM((2, 4, 2, 32, 512), BF),
            pltpu.VMEM((16, 32, 512), BF),
            dma((4,)), dma((2, 4)), dma((2, 4)), dma((2,)), dma((2,)), dma((2,)), dma((2,)),
            dma((3, 32)), dma((3, 32)), dma((12,)), dma((12,)), dma((4,)), dma((4,)),
            dma((NC, 6)), dma((NC, 6)), dma((NC, 32)), dma((NC, 32)),
            dma((2,)), dma((2,)), dma((2, 4, 2)), dma((16,)),
        ],
        compiler_params=pltpu.CompilerParams(
            collective_id=0, has_side_effects=True, vmem_limit_bytes=56 * 1024 * 1024
        ),
        cost_estimate=pl.CostEstimate(flops=4 * 2**30, bytes_accessed=12 * 2**20, transcendentals=2**18),
    )(
        inverse, new_map, counts,
        old_master.reshape(128, 2048), old_moment.reshape(128, 2048), old_second.reshape(128, 2048),
        tokens_in, upstream,
    )
    pieces = pieces.reshape(3, 1, 1, 256, 1024).astype(F32)
    return pieces[0], pieces[1], pieces[2], input_grad


def solution(mesh):
    pieces = P("tensor", "dp", None, None)
    return jax.shard_map(
        shards,
        mesh=mesh,
        in_specs=(pieces, pieces, pieces, P("dp", None), P("dp", "tensor"), P(), P(), P()),
        out_specs=(pieces, pieces, pieces, P("dp", "tensor")),
        check_vma=False,
    )
```

```python
import jax
import jax.numpy as jnp
from jax import lax
from jax.experimental import pallas as pl
from jax.experimental.pallas import tpu as pltpu
from jax.sharding import PartitionSpec as P

beta_first = 0.9
beta_second = 0.95
learn_rate = 0.05
decay_rate = 0.1
epsilon = 1e-08

BF = jnp.bfloat16
F32 = jnp.float32
NT = (((1,), (1,)), ((), ()))
NC = 2
PER = NC // 2
RR = 32 // PER
CT = F32


def kernel(
    map_ref, new_ref, cnt_ref, om_ref, oo_ref, os_ref, tok_ref, up_ref,
    out_ref, ig_ref,
    inv_ref, old, tok, send1, spread_a, spread_b, spread_c, gath, lhs, tsend, acc, part, r1, r2, wg,
    upd, send2, cpart, crecv, csum, cfin,
    ld, us, ur, es, er, ts, tr, p1s, p1r, xs, xr, ws, wr, rs, rr, p2s, p2r, ks, kr, cs, cr,
):
    spread = (spread_a, spread_b, spread_c)
    g = lax.axis_index("dp")
    t = lax.axis_index("tensor")
    zl, y = g // 4, g % 4
    z, x, k = t // 8, (t // 2) % 4, t % 2
    zp = 1 - zl
    y_up, y_dn, y_far = (y + 1) % 4, (y + 3) % 4, (y + 2) % 4
    g_up, g_dn, g_pair = zl * 4 + y_up, zl * 4 + y_dn, zp * 4 + y
    x_up, x_dn, x_far = (x + 1) % 4, (x + 3) % 4, (x + 2) % 4
    t_xup, t_xdn = z * 8 + x_up * 2 + k, z * 8 + x_dn * 2 + k
    t_core = z * 8 + x * 2 + 1 - k

    def remote(src, dst, ssem, rsem, dp, tn):
        return pltpu.make_async_remote_copy(
            src_ref=src, dst_ref=dst, send_sem=ssem, recv_sem=rsem,
            device_id=(dp, tn), device_id_type=pl.DeviceIdType.MESH,
        )

    def cols(index, width):
        return pl.ds(pl.multiple_of(index * width, width), width)

    def spread_out(n):
        return (n % 4) * 8 + n // 4

    sent = []

    def start(*copies):
        for c in copies:
            c.start()
            sent.append(c)

    loads = [
        pltpu.make_async_copy(src, old.at[a], ld.at[a]) for a, src in enumerate((om_ref, oo_ref, os_ref))
    ] + [pltpu.make_async_copy(tok_ref, tok, ld.at[3])]
    for c in loads:
        c.start()

    barrier = pltpu.get_barrier_semaphore()

    def greet(j, c):
        pl.semaphore_signal(barrier, inc=1, device_id=(g, (t + j) % 32), device_id_type=pl.DeviceIdType.MESH)
        return c

    lax.fori_loop(1, 32, greet, 0)
    for other in (g_up, g_dn):
        pl.semaphore_signal(barrier, inc=1, device_id=(other, t), device_id_type=pl.DeviceIdType.MESH)

    def greet_pair(j, c):
        pl.semaphore_signal(barrier, inc=1, device_id=(g_pair, j * 2 + k), device_id_type=pl.DeviceIdType.MESH)
        return c

    lax.fori_loop(0, 16, greet_pair, 0)

    def narrow(a):
        loads[a].wait()

        def body(i, c):
            c10, xx = i // 4, i % 4
            send1[a, c10, xx] = old[a, cols(xx, 32), cols(c10, 1024)].astype(BF)
            return c

        lax.fori_loop(0, 8, body, 0)

    near = 1 + 2 * zl
    z_near, z_other, z_far = (z + 4 - near) % 4, (z + near) % 4, (z + 2) % 4
    own_blocks = ((zl, z), (zl, z_near), (zp, z_near), (zp, z_far))
    pair_blocks = ((zp, z), (zp, z_other), (zl, z_other), (zl, z_far))

    def place_of(zz, zs, xx):
        return gath.at[cols(zz, 512), cols(xx * 4 + zs, 128)]

    def u1(dz):
        to = (z + dz) % 4
        lo, at = {1: (0, 1 + zl), 3: (1, 2 - zl), 2: (zp, 3)}[dz]
        return remote(
            up_ref.at[:, cols(to, 128)], place_of(zl, z, x), us.at[dz], ur.at[at], lo * 4 + y, to * 8 + x * 2 + k
        )

    def u1_in(n):
        return remote(up_ref.at[:, cols(z, 128)], place_of(*own_blocks[n], x), us.at[n], ur.at[n], g, t_core)

    u1_own = pltpu.make_async_copy(up_ref.at[:, cols(z, 128)], place_of(zl, z, x), ur.at[0])

    def u2(n):
        ref = place_of(*own_blocks[n], x)
        return remote(ref, ref, es.at[n], er.at[n], g_pair, t)

    def u2_in(n):
        ref = place_of(*pair_blocks[n], x)
        return remote(ref, ref, es.at[n], er.at[n], g_pair, t)

    def invert(piece, c):
        slot = jnp.int32(0)
        for s in range(1, 32):
            slot = jnp.where(map_ref[s] == piece, jnp.int32(s), slot)
        inv_ref[piece] = slot
        return c

    def p1(a, j):
        p = (t + j) % 32
        pz, px, pk = p // 8, (p // 2) % 4, p % 2
        return remote(
            send1.at[a, :, px, :, cols(pk * 4 + pz, 128)], spread[a].at[t],
            p1s.at[a, j], p1r.at[a, j], g, p,
        )

    def p1_in(a, j):
        return remote(
            send1.at[a, :, x, :, cols(k * 4 + z, 128)], spread[a].at[(t + 32 - j) % 32],
            p1s.at[a, j], p1r.at[a, j], g, t_core,
        )

    def p1_own(a):
        return pltpu.make_async_copy(send1.at[a, :, x, :, cols(k * 4 + z, 128)], spread[a].at[t], p1r.at[a, 0])

    def p1_start(a):
        p1_own(a).start()

        def body(n, c):
            p1(a, spread_out(n)).start()
            return c

        lax.fori_loop(1, 32, body, 0)

    def p1_wait(a):
        p1_own(a).wait()

        def body(j, c):
            p1_in(a, j).wait_recv()
            return c

        lax.fori_loop(1, 32, body, 0)

    live = cnt_ref[g]
    pick_row = lax.broadcasted_iota(jnp.int32, (128, 512), 0)
    pick_col = lax.broadcasted_iota(jnp.int32, (128, 512), 1)
    chunk_of, so1_of = pick_row // (2 * RR), (pick_row // RR) % 2
    so_of = so1_of * 2 + chunk_of // PER
    r_of = (chunk_of % PER) * RR + pick_row % RR
    pick = jnp.where(pick_col == so_of * 128 + x * 32 + r_of, 1.0, 0.0).astype(BF)
    alive = lax.broadcasted_iota(jnp.int32, (128, 512), 1) < live

    def transpose_tokens(yy, c):
        for zz, ref, where in ((zl, lhs, cols(zl, 512)), (zp, tsend, pl.ds(0, 512))):
            rows = lax.dot_general(pick, tok[:, cols(zz * 4 + yy, 512)], NT, preferred_element_type=F32)
            rows = jnp.where(alive, rows, 0.0).astype(BF)
            for i in range(NC):
                ref[cols(i * 4 + yy, 2 * RR), where] = rows[i * 2 * RR : (i + 1) * 2 * RR]
        return c

    def tokens_pair(zz, kk):
        rows = cols(kk, 256)
        return remote(tsend.at[rows], lhs.at[rows, cols(zz, 512)], ts.at[0], tr.at[0], g_pair, t)

    def tokens_core(kk):
        ref = lhs.at[cols(kk, 256), cols(zp, 512)]
        return remote(ref, ref, ts.at[1], tr.at[1], g, t_core)

    blocks = own_blocks + pair_blocks

    def x_copy(n, xx, rows, way, sem):
        zz, zs = blocks[n]
        ref = gath.at[pl.ds(pl.multiple_of(zz * 512 + rows[0], 256), rows[1]), cols(xx * 4 + zs, 128)]
        return remote(ref, ref, xs.at[n, sem], xr.at[n, sem], g, way)

    whole, top, bottom = (0, 512), (0, 256), (256, 256)

    def x_near(n):
        start(x_copy(n, x, whole, t_xup, 0), x_copy(n, x, whole, t_xdn, 1))

    def x_relay(n):
        x_copy(n, x_dn, whole, t_xup, 0).wait_recv()
        start(x_copy(n, x_dn, top, t_xup, 2))
        x_copy(n, x_up, whole, t_xdn, 1).wait_recv()
        start(x_copy(n, x_up, bottom, t_xdn, 3))

    def x_wait(n):
        x_copy(n, x_far, top, t_xup, 2).wait_recv()
        x_copy(n, x_far, bottom, t_xdn, 3).wait_recv()

    def own_in(n):
        if n == 0:
            u1_own.wait()
        else:
            u1_in(n).wait_recv()
        start(u2(n))
        x_near(n)

    def pair_in(n):
        u2_in(n).wait_recv()
        x_near(4 + n)

    def place(q):
        zs, half = q % 4, q // 4
        return zs * 2 + half // 2, half % 2

    def weights(q, c):
        bo, c10 = place(q)
        for so in range(4):
            wg[cols(y * 4 + so, 32), cols(q, 128)] = spread[0][inv_ref[bo * 4 + so], c10]
        return c

    def ring_w(yy, start_row, rows, to, sem):
        ref = wg.at[pl.ds(pl.multiple_of(yy * 128 + start_row, 64), rows), :]
        return remote(ref, ref, ws.at[sem], wr.at[sem], to, t)

    def block(i, yy, so1):
        return part.at[cols(i * 8 + yy * 2 + so1, RR), :]

    def partial(zz):
        def body(c, carry):
            here = cols(c, 512)
            product = jnp.dot(
                lhs[:, cols(zz, 512)], gath[cols(zz, 512), here], preferred_element_type=F32
            )
            if zz is zl:
                acc[:, here] = product
            else:
                part[:, here] = (acc[:, here] + product).astype(BF)
            return carry

        lax.fori_loop(0, 4, body, 0)

    def sum_copy(i, n, src, dst, to):
        return remote(src, dst, rs.at[i, n], rr.at[i, n], to, t)

    def far_up(i):
        return sum_copy(i, 0, block(i, y_far, 0), r1.at[i, 0], g_up)

    def far_dn(i):
        return sum_copy(i, 1, block(i, y_far, 1), r1.at[i, 1], g_dn)

    def near_up(i, so1):
        return sum_copy(i, 2 + so1, block(i, y_up, so1), r2.at[i, 0, so1], g_up)

    def near_dn(i, so1):
        return sum_copy(i, 4 + so1, block(i, y_dn, so1), r2.at[i, 1, so1], g_dn)

    def add_into(i, yy, so1):
        at = cols(i * 8 + yy * 2 + so1, RR)
        part[at, :] = (part[at, :].astype(F32) + r1[i, so1].astype(F32)).astype(BF)

    def sum_first(i):
        start(far_up(i), far_dn(i), near_up(i, 1), near_dn(i, 0))

    def sum_second(i):
        far_up(i).wait_recv()
        add_into(i, y_up, 0)
        start(near_up(i, 0))
        far_dn(i).wait_recv()
        add_into(i, y_dn, 1)
        start(near_dn(i, 1))

    fix_first = 1.0 - beta_first**10
    fix_second = 1.0 - beta_second**10
    scale = 1.0 / 64.0

    def adamw(i):
        for so1 in range(2):
            near_up(i, so1).wait_recv()
            near_dn(i, so1).wait_recv()
        so0, r0 = i // PER, (i % PER) * RR

        def body(zs, carry):
            done = []
            for xs in range(4):
                bo, c10 = zs * 2 + xs // 2, xs % 2
                here = cols(xs * 4 + zs, 128)
                for so1 in range(2):
                    slot = inv_ref[bo * 4 + so1 * 2 + so0]
                    mine = cols(i * 8 + y * 2 + so1, RR)
                    grad = part[mine, here].astype(F32) + r2[i, 0, so1, :, here].astype(F32)
                    grad = (grad + r2[i, 1, so1, :, here].astype(F32)) * scale
                    rows = slice(r0, r0 + RR)
                    master = spread[0][slot, c10, rows].astype(F32)
                    moment = beta_first * spread[1][slot, c10, rows].astype(F32) + (1.0 - beta_first) * grad
                    second = beta_second * spread[2][slot, c10, rows].astype(F32) + (1.0 - beta_second) * grad * grad
                    root = jnp.sqrt(second * (1.0 / fix_second)) + epsilon
                    update = moment * (1.0 / fix_first) / root + decay_rate * master
                    piece = (bo * 2 + c10) * 2 + so1
                    done.append((piece, master - learn_rate * update, moment, second))
            for piece, *values in done:
                for a, value in enumerate(values):
                    upd[i, piece, a] = value.astype(BF)
            return carry

        lax.fori_loop(0, 4, body, 0)

    def p2_place(i, px, pk, pz):
        return out_ref.at[:, i // PER, px, pl.ds((i % PER) * RR, RR), cols(pk * 4 + pz, 128)]

    def p2(i, j):
        p = (t + j) % 32
        return remote(send2[i].at[p], p2_place(i, x, k, z), p2s.at[i, j], p2r.at[i, j], g, p)

    def p2_in(i, j):
        p = (t + 32 - j) % 32
        return remote(
            send2[i].at[t], p2_place(i, (p // 2) % 4, p % 2, p // 8), p2s.at[i, j], p2r.at[i, j], g, t_core
        )

    def p2_own(i):
        return pltpu.make_async_copy(send2[i].at[t], p2_place(i, x, k, z), p2r.at[i, 0])

    def p2_start(i):
        def select(j, carry):
            for u in range(4):
                send2[i][j * 4 + u] = upd[i, new_ref[j * 4 + u]]
            return carry

        lax.fori_loop(0, 8, select, 0)

        def body(n, carry):
            p2(i, spread_out(n)).start()
            return carry

        lax.fori_loop(1, 32, body, 0)
        p2_own(i).start()

    def back(tz):
        def body(c, carry):
            rows = lax.dot_general(
                wg[...], gath[cols(tz * 2 + c, 256), :], NT, preferred_element_type=F32
            )
            for yy in range(4):
                for so in range(4):
                    at = yy * 128 + so * 32
                    cpart[tz, yy, so // 2, so % 2, :, cols(c, 256)] = rows[at : at + 32].astype(CT)
            return carry

        lax.fori_loop(0, 2, body, 0)

    def core_copy(tz):
        at = 0 if tz is zl else 1
        return remote(cpart.at[tz, :, :, 1 - k], crecv.at[tz], ks.at[at], kr.at[at], g, t_core)

    def back_send(tz):
        back(tz)
        start(core_copy(tz))

    me16 = z * 4 + x
    c_own = pltpu.make_async_copy(csum.at[zl, (z % 2) * 2 + x // 2, x % 2], cfin.at[me16], cr.at[me16])

    def c_parts(tz):
        for yy in range(4):
            for so1 in range(2):
                pz, px = zl * 2 + yy // 2, (yy % 2) * 2 + so1
                here = jnp.logical_and(pz == z, px == x)
                copy = remote(
                    csum.at[tz, yy, so1], cfin.at[me16], cs.at[0 if tz is zl else 1, yy, so1], cr.at[me16],
                    tz * 4 + y, pz * 8 + px * 2 + k,
                )
                yield here, copy

    def back_sum(tz):
        core_copy(tz).wait_recv()

        def body(yy, carry):
            csum[tz, yy] = (cpart[tz, yy, :, k].astype(F32) + crecv[tz, yy].astype(F32)).astype(BF)
            return carry

        lax.fori_loop(0, 4, body, 0)
        for here, copy in c_parts(tz):
            if tz is zl:

                @pl.when(jnp.logical_not(here))
                def _():
                    copy.start()

                @pl.when(here)
                def _():
                    c_own.start()

            else:
                start(copy)

    narrow(0)
    pl.semaphore_wait(barrier, 49)
    u1_own.start()
    for dz in (2, 1, 3):
        start(u1(dz))
    own_in(0)
    narrow(1)
    narrow(2)
    own_in(1)
    p1_start(0)
    own_in(2)
    own_in(3)
    p1_start(1)
    loads[3].wait()
    lax.fori_loop(0, 4, transpose_tokens, 0)
    start(tokens_pair(zl, k))
    x_relay(0)
    x_relay(1)
    pair_in(2)
    pair_in(3)
    lax.fori_loop(0, 32, invert, 0)
    p1_wait(0)
    lax.fori_loop(0, 16, weights, 0)
    start(ring_w(y, 0, 128, g_up, 0), ring_w(y, 0, 128, g_dn, 1))
    p1_start(2)
    pair_in(0)
    pair_in(1)
    x_relay(2)
    x_relay(3)
    x_relay(6)
    x_relay(7)
    tokens_pair(zp, k).wait_recv()
    start(tokens_core(k))
    ring_w(y_dn, 0, 128, g_up, 0).wait_recv()
    start(ring_w(y_dn, 0, 64, g_up, 2))
    ring_w(y_up, 0, 128, g_dn, 1).wait_recv()
    start(ring_w(y_up, 64, 64, g_dn, 3))
    x_relay(4)
    x_relay(5)
    x_wait(0)
    x_wait(1)
    x_wait(6)
    x_wait(7)
    partial(zl)
    ring_w(y_far, 0, 64, g_up, 2).wait_recv()
    ring_w(y_far, 64, 64, g_dn, 3).wait_recv()
    back_send(zl)
    x_wait(2)
    x_wait(3)
    x_wait(4)
    x_wait(5)
    tokens_core(1 - k).wait_recv()
    partial(zp)
    sum_first(0)
    back_sum(zl)
    sum_second(0)
    sum_first(1)
    p1_wait(1)
    p1_wait(2)
    adamw(0)
    p2_start(0)
    back_send(zp)
    sum_second(1)
    back_sum(zp)
    adamw(1)
    p2_start(1)

    def c_wait(j, carry):
        remote(csum.at[0, 0, 0], cfin.at[j], cs.at[0, 0, 0], cr.at[j], g, t_core).wait_recv()
        return carry

    lax.fori_loop(0, 16, c_wait, 0)
    token = lax.broadcasted_iota(jnp.int32, (512, 128), 0)
    sums = []
    for xx in range(4):
        total = cfin[xx].astype(F32) + cfin[4 + xx].astype(F32)
        sums.append(total + cfin[8 + xx].astype(F32) + cfin[12 + xx].astype(F32))
    full = jnp.concatenate(sums, axis=0) * scale
    ig_ref[...] = jnp.where(token < live, full.T, 0.0).astype(BF)

    for i in range(NC):
        p2_own(i).wait()

        def p2_wait(j, carry):
            p2_in(i, j).wait_recv()
            p2(i, j).wait_send()
            return carry

        lax.fori_loop(1, 32, p2_wait, 0)

    for here, copy in c_parts(zl):

        @pl.when(jnp.logical_not(here))
        def _():
            copy.wait_send()


    def p1_sent(j, carry):
        for a in range(3):
            p1(a, j).wait_send()
        return carry

    lax.fori_loop(1, 32, p1_sent, 0)
    for c in sent:
        c.wait_send()


def shards(old_master, old_moment, old_second, tokens_in, upstream, counts, old_map, new_map):
    hbm = pl.BlockSpec(memory_space=pl.ANY)
    smem = pl.BlockSpec(memory_space=pltpu.SMEM)
    vmem = pl.BlockSpec(memory_space=pltpu.VMEM)
    dma = pltpu.SemaphoreType.DMA
    pieces, input_grad = pl.pallas_call(
        kernel,
        out_shape=(
            jax.ShapeDtypeStruct((3, 2, 4, 32, 1024), BF),
            jax.ShapeDtypeStruct((512, 128), BF),
        ),
        in_specs=[smem] * 3 + [hbm] * 5,
        out_specs=(vmem, vmem),
        scratch_shapes=[
            pltpu.SMEM((32,), jnp.int32),
            pltpu.VMEM((3, 128, 2048), F32),
            pltpu.VMEM((512, 4096), BF),
            pltpu.VMEM((3, 2, 4, 32, 1024), BF),
            pltpu.VMEM((32, 2, 32, 128), BF),
            pltpu.VMEM((32, 2, 32, 128), BF),
            pltpu.VMEM((32, 2, 32, 128), BF),
            pltpu.VMEM((1024, 2048), BF),
            pltpu.VMEM((512, 1024), BF),
            pltpu.VMEM((512, 512), BF),
            pltpu.VMEM((512, 2048), F32),
            pltpu.VMEM((512, 2048), BF),
            pltpu.VMEM((NC, 2, RR, 2048), BF),
            pltpu.VMEM((NC, 2, 2, RR, 2048), BF),
            pltpu.VMEM((512, 2048), BF),
            pltpu.VMEM((NC, 32, 3, RR, 128), BF),
            [pltpu.VMEM((32, 3, RR, 128), BF)] * NC,
            pltpu.VMEM((2, 4, 2, 2, 32, 512), CT),
            pltpu.VMEM((2, 4, 2, 32, 512), CT),
            pltpu.VMEM((2, 4, 2, 32, 512), BF),
            pltpu.VMEM((16, 32, 512), BF),
            dma((4,)), dma((4,)), dma((4,)), dma((4,)), dma((4,)), dma((2,)), dma((2,)),
            dma((3, 32)), dma((3, 32)), dma((8, 4)), dma((8, 4)), dma((4,)), dma((4,)),
            dma((NC, 6)), dma((NC, 6)), dma((NC, 32)), dma((NC, 32)),
            dma((2,)), dma((2,)), dma((2, 4, 2)), dma((16,)),
        ],
        compiler_params=pltpu.CompilerParams(
            collective_id=0, has_side_effects=True, vmem_limit_bytes=56 * 1024 * 1024
        ),
        cost_estimate=pl.CostEstimate(flops=4 * 2**30, bytes_accessed=12 * 2**20, transcendentals=2**18),
    )(
        old_map, new_map, counts,
        old_master.reshape(128, 2048), old_moment.reshape(128, 2048), old_second.reshape(128, 2048),
        tokens_in, upstream,
    )
    pieces = pieces.reshape(3, 1, 1, 256, 1024).astype(F32)
    return pieces[0], pieces[1], pieces[2], input_grad


def solution(mesh):
    pieces = P("tensor", "dp", None, None)
    return jax.shard_map(
        shards,
        mesh=mesh,
        in_specs=(pieces, pieces, pieces, P("dp", None), P("dp", "tensor"), P(), P(), P()),
        out_specs=(pieces, pieces, pieces, P("dp", "tensor")),
        check_vma=False,
    )
```

```python
import jax
import jax.numpy as jnp
from jax import lax
from jax.experimental import pallas as pl
from jax.experimental.pallas import tpu as pltpu
from jax.sharding import PartitionSpec as P

beta_first = 0.9
beta_second = 0.95
learn_rate = 0.05
decay_rate = 0.1
epsilon = 1e-08

BF = jnp.bfloat16
F32 = jnp.float32
NT = (((1,), (1,)), ((), ()))
NC = 2
PER = NC // 2
RR = 32 // PER
CT = F32


def kernel(
    map_ref, new_ref, cnt_ref, om_ref, oo_ref, os_ref, tok_ref, up_ref,
    out_ref, ig_ref,
    inv_ref, old, tok, send1, spread_a, spread_b, spread_c, gath, lhs, tsend, acc, part, r1, r2, wg,
    upd, send2, cpart, crecv, csum, cfin,
    ld, us, ur, es, er, ts, tr, p1s, p1r, xs, xr, ws, wr, rs, rr, p2s, p2r, ks, kr, cs, cr,
):
    spread = (spread_a, spread_b, spread_c)
    g = lax.axis_index("dp")
    t = lax.axis_index("tensor")
    zl, y = g // 4, g % 4
    z, x, k = t // 8, (t // 2) % 4, t % 2
    zp = 1 - zl
    y_up, y_dn, y_far = (y + 1) % 4, (y + 3) % 4, (y + 2) % 4
    g_up, g_dn, g_pair = zl * 4 + y_up, zl * 4 + y_dn, zp * 4 + y
    x_up, x_dn, x_far = (x + 1) % 4, (x + 3) % 4, (x + 2) % 4
    t_xup, t_xdn = z * 8 + x_up * 2 + k, z * 8 + x_dn * 2 + k
    t_core = z * 8 + x * 2 + 1 - k

    def remote(src, dst, ssem, rsem, dp, tn):
        return pltpu.make_async_remote_copy(
            src_ref=src, dst_ref=dst, send_sem=ssem, recv_sem=rsem,
            device_id=(dp, tn), device_id_type=pl.DeviceIdType.MESH,
        )

    def cols(index, width):
        return pl.ds(pl.multiple_of(index * width, width), width)

    def spread_out(n):
        return (n % 4) * 8 + n // 4

    sent = []

    def start(*copies):
        for c in copies:
            c.start()
            sent.append(c)

    loads = [
        pltpu.make_async_copy(src, old.at[a], ld.at[a]) for a, src in enumerate((om_ref, oo_ref, os_ref))
    ] + [pltpu.make_async_copy(tok_ref, tok, ld.at[3])]
    for c in loads:
        c.start()

    barrier = pltpu.get_barrier_semaphore()

    def greet(j, c):
        pl.semaphore_signal(barrier, inc=1, device_id=(g, (t + j) % 32), device_id_type=pl.DeviceIdType.MESH)
        return c

    lax.fori_loop(1, 32, greet, 0)
    for other in (g_up, g_dn):
        pl.semaphore_signal(barrier, inc=1, device_id=(other, t), device_id_type=pl.DeviceIdType.MESH)

    def greet_pair(j, c):
        pl.semaphore_signal(barrier, inc=1, device_id=(g_pair, j * 2 + k), device_id_type=pl.DeviceIdType.MESH)
        return c

    lax.fori_loop(0, 16, greet_pair, 0)

    def narrow(a):
        loads[a].wait()

        def body(i, c):
            c10, xx = i // 4, i % 4
            send1[a, c10, xx] = old[a, cols(xx, 32), cols(c10, 1024)].astype(BF)
            return c

        lax.fori_loop(0, 8, body, 0)

    near = 1 + 2 * zl
    z_near, z_other, z_far = (z + 4 - near) % 4, (z + near) % 4, (z + 2) % 4
    own_blocks = ((zl, z), (zl, z_near), (zp, z_near), (zp, z_far))
    pair_blocks = ((zp, z), (zp, z_other), (zl, z_other), (zl, z_far))

    def place_of(zz, zs, xx):
        return gath.at[cols(zz, 512), cols(xx * 4 + zs, 128)]

    def u1(dz):
        to = (z + dz) % 4
        lo, at = {1: (0, 1 + zl), 3: (1, 2 - zl), 2: (zp, 3)}[dz]
        return remote(
            up_ref.at[:, cols(to, 128)], place_of(zl, z, x), us.at[dz], ur.at[at], lo * 4 + y, to * 8 + x * 2 + k
        )

    def u1_in(n):
        return remote(up_ref.at[:, cols(z, 128)], place_of(*own_blocks[n], x), us.at[n], ur.at[n], g, t_core)

    u1_own = pltpu.make_async_copy(up_ref.at[:, cols(z, 128)], place_of(zl, z, x), ur.at[0])

    def u2(n):
        ref = place_of(*own_blocks[n], x)
        return remote(ref, ref, es.at[n], er.at[n], g_pair, t)

    def u2_in(n):
        ref = place_of(*pair_blocks[n], x)
        return remote(ref, ref, es.at[n], er.at[n], g_pair, t)

    def invert(piece, c):
        slot = jnp.int32(0)
        for s in range(1, 32):
            slot = jnp.where(map_ref[s] == piece, jnp.int32(s), slot)
        inv_ref[piece] = slot
        return c

    def p1(a, j):
        p = (t + j) % 32
        pz, px, pk = p // 8, (p // 2) % 4, p % 2
        return remote(
            send1.at[a, :, px, :, cols(pk * 4 + pz, 128)], spread[a].at[t],
            p1s.at[a, j], p1r.at[a, j], g, p,
        )

    def p1_in(a, j):
        return remote(
            send1.at[a, :, x, :, cols(k * 4 + z, 128)], spread[a].at[(t + 32 - j) % 32],
            p1s.at[a, j], p1r.at[a, j], g, t_core,
        )

    def p1_own(a):
        return pltpu.make_async_copy(send1.at[a, :, x, :, cols(k * 4 + z, 128)], spread[a].at[t], p1r.at[a, 0])

    def p1_start(a):
        p1_own(a).start()

        def body(n, c):
            p1(a, spread_out(n)).start()
            return c

        lax.fori_loop(1, 32, body, 0)

    def p1_wait(a):
        p1_own(a).wait()

        def body(j, c):
            p1_in(a, j).wait_recv()
            return c

        lax.fori_loop(1, 32, body, 0)

    live = cnt_ref[g]
    pick_row = lax.broadcasted_iota(jnp.int32, (128, 512), 0)
    pick_col = lax.broadcasted_iota(jnp.int32, (128, 512), 1)
    chunk_of, so1_of = pick_row // (2 * RR), (pick_row // RR) % 2
    so_of = so1_of * 2 + chunk_of // PER
    r_of = (chunk_of % PER) * RR + pick_row % RR
    pick = jnp.where(pick_col == so_of * 128 + x * 32 + r_of, 1.0, 0.0).astype(BF)
    alive = lax.broadcasted_iota(jnp.int32, (128, 512), 1) < live

    def transpose_tokens(yy, c):
        for zz, ref, where in ((zl, lhs, cols(zl, 512)), (zp, tsend, pl.ds(0, 512))):
            rows = lax.dot_general(pick, tok[:, cols(zz * 4 + yy, 512)], NT, preferred_element_type=F32)
            rows = jnp.where(alive, rows, 0.0).astype(BF)
            for i in range(NC):
                ref[cols(i * 4 + yy, 2 * RR), where] = rows[i * 2 * RR : (i + 1) * 2 * RR]
        return c

    def tokens_pair(zz, kk):
        rows = cols(kk, 256)
        return remote(tsend.at[rows], lhs.at[rows, cols(zz, 512)], ts.at[0], tr.at[0], g_pair, t)

    def tokens_core(kk):
        ref = lhs.at[cols(kk, 256), cols(zp, 512)]
        return remote(ref, ref, ts.at[1], tr.at[1], g, t_core)

    blocks = own_blocks + pair_blocks

    def x_copy(n, xx, rows, way, sem):
        zz, zs = blocks[n]
        ref = gath.at[pl.ds(pl.multiple_of(zz * 512 + rows[0], 256), rows[1]), cols(xx * 4 + zs, 128)]
        return remote(ref, ref, xs.at[n, sem], xr.at[n, sem], g, way)

    whole, top, bottom = (0, 512), (0, 256), (256, 256)

    def x_near(n):
        start(x_copy(n, x, whole, t_xup, 0), x_copy(n, x, whole, t_xdn, 1))

    def x_relay(n):
        x_copy(n, x_dn, whole, t_xup, 0).wait_recv()
        start(x_copy(n, x_dn, top, t_xup, 2))
        x_copy(n, x_up, whole, t_xdn, 1).wait_recv()
        start(x_copy(n, x_up, bottom, t_xdn, 3))

    def x_wait(n):
        x_copy(n, x_far, top, t_xup, 2).wait_recv()
        x_copy(n, x_far, bottom, t_xdn, 3).wait_recv()

    def own_in(n):
        if n == 0:
            u1_own.wait()
        else:
            u1_in(n).wait_recv()
        start(u2(n))
        x_near(n)

    def pair_in(n):
        u2_in(n).wait_recv()
        x_near(4 + n)

    def place(q):
        zs, half = q % 4, q // 4
        return zs * 2 + half // 2, half % 2

    def weights(q, c):
        bo, c10 = place(q)
        for so in range(4):
            wg[cols(y * 4 + so, 32), cols(q, 128)] = spread[0][inv_ref[bo * 4 + so], c10]
        return c

    def ring_w(yy, start_row, rows, to, sem):
        ref = wg.at[pl.ds(pl.multiple_of(yy * 128 + start_row, 64), rows), :]
        return remote(ref, ref, ws.at[sem], wr.at[sem], to, t)

    def block(i, yy, so1):
        return part.at[cols(i * 8 + yy * 2 + so1, RR), :]

    def partial(zz):
        def body(c, carry):
            here = cols(c, 512)
            product = jnp.dot(
                lhs[:, cols(zz, 512)], gath[cols(zz, 512), here], preferred_element_type=F32
            )
            if zz is zl:
                acc[:, here] = product
            else:
                part[:, here] = (acc[:, here] + product).astype(BF)
            return carry

        lax.fori_loop(0, 4, body, 0)

    def sum_copy(i, n, src, dst, to):
        return remote(src, dst, rs.at[i, n], rr.at[i, n], to, t)

    def far_up(i):
        return sum_copy(i, 0, block(i, y_far, 0), r1.at[i, 0], g_up)

    def far_dn(i):
        return sum_copy(i, 1, block(i, y_far, 1), r1.at[i, 1], g_dn)

    def near_up(i, so1):
        return sum_copy(i, 2 + so1, block(i, y_up, so1), r2.at[i, 0, so1], g_up)

    def near_dn(i, so1):
        return sum_copy(i, 4 + so1, block(i, y_dn, so1), r2.at[i, 1, so1], g_dn)

    def add_into(i, yy, so1):
        at = cols(i * 8 + yy * 2 + so1, RR)
        part[at, :] = (part[at, :].astype(F32) + r1[i, so1].astype(F32)).astype(BF)

    def sum_first(i):
        start(far_up(i), far_dn(i), near_up(i, 1), near_dn(i, 0))

    def sum_second(i):
        far_up(i).wait_recv()
        add_into(i, y_up, 0)
        start(near_up(i, 0))
        far_dn(i).wait_recv()
        add_into(i, y_dn, 1)
        start(near_dn(i, 1))

    fix_first = 1.0 - beta_first**10
    fix_second = 1.0 - beta_second**10
    scale = 1.0 / 64.0

    def adamw(i):
        for so1 in range(2):
            near_up(i, so1).wait_recv()
            near_dn(i, so1).wait_recv()
        so0, r0 = i // PER, (i % PER) * RR

        def body(zs, carry):
            done = []
            for xs in range(4):
                bo, c10 = zs * 2 + xs // 2, xs % 2
                here = cols(xs * 4 + zs, 128)
                for so1 in range(2):
                    slot = inv_ref[bo * 4 + so1 * 2 + so0]
                    mine = cols(i * 8 + y * 2 + so1, RR)
                    grad = part[mine, here].astype(F32) + r2[i, 0, so1, :, here].astype(F32)
                    grad = (grad + r2[i, 1, so1, :, here].astype(F32)) * scale
                    rows = slice(r0, r0 + RR)
                    master = spread[0][slot, c10, rows].astype(F32)
                    moment = beta_first * spread[1][slot, c10, rows].astype(F32) + (1.0 - beta_first) * grad
                    second = beta_second * spread[2][slot, c10, rows].astype(F32) + (1.0 - beta_second) * grad * grad
                    root = jnp.sqrt(second * (1.0 / fix_second)) + epsilon
                    update = moment * (1.0 / fix_first) / root + decay_rate * master
                    piece = (bo * 2 + c10) * 2 + so1
                    done.append((piece, master - learn_rate * update, moment, second))
            for piece, *values in done:
                for a, value in enumerate(values):
                    upd[i, piece, a] = value.astype(BF)
            return carry

        lax.fori_loop(0, 4, body, 0)

    def p2_place(i, px, pk, pz):
        return out_ref.at[:, i // PER, px, pl.ds((i % PER) * RR, RR), cols(pk * 4 + pz, 128)]

    def p2(i, j):
        p = (t + j) % 32
        return remote(send2[i].at[p], p2_place(i, x, k, z), p2s.at[i, j], p2r.at[i, j], g, p)

    def p2_in(i, j):
        p = (t + 32 - j) % 32
        return remote(
            send2[i].at[t], p2_place(i, (p // 2) % 4, p % 2, p // 8), p2s.at[i, j], p2r.at[i, j], g, t_core
        )

    def p2_own(i):
        return pltpu.make_async_copy(send2[i].at[t], p2_place(i, x, k, z), p2r.at[i, 0])

    def p2_start(i):
        def select(j, carry):
            for u in range(4):
                send2[i][j * 4 + u] = upd[i, new_ref[j * 4 + u]]
            return carry

        lax.fori_loop(0, 8, select, 0)

        def body(n, carry):
            p2(i, spread_out(n)).start()
            return carry

        lax.fori_loop(1, 32, body, 0)
        p2_own(i).start()

    def back(tz):
        def body(c, carry):
            rows = lax.dot_general(
                wg[...], gath[cols(tz * 2 + c, 256), :], NT, preferred_element_type=F32
            )
            for yy in range(4):
                for so in range(4):
                    at = yy * 128 + so * 32
                    cpart[tz, yy, so // 2, so % 2, :, cols(c, 256)] = rows[at : at + 32].astype(CT)
            return carry

        lax.fori_loop(0, 2, body, 0)

    def core_copy(tz):
        at = 0 if tz is zl else 1
        return remote(cpart.at[tz, :, :, 1 - k], crecv.at[tz], ks.at[at], kr.at[at], g, t_core)

    def back_send(tz):
        back(tz)
        start(core_copy(tz))

    me16 = z * 4 + x
    c_own = pltpu.make_async_copy(csum.at[zl, (z % 2) * 2 + x // 2, x % 2], cfin.at[me16], cr.at[me16])

    def c_parts(tz):
        for yy in range(4):
            for so1 in range(2):
                pz, px = zl * 2 + yy // 2, (yy % 2) * 2 + so1
                here = jnp.logical_and(pz == z, px == x)
                copy = remote(
                    csum.at[tz, yy, so1], cfin.at[me16], cs.at[0 if tz is zl else 1, yy, so1], cr.at[me16],
                    tz * 4 + y, pz * 8 + px * 2 + k,
                )
                yield here, copy

    def back_sum(tz):
        core_copy(tz).wait_recv()

        def body(yy, carry):
            csum[tz, yy] = (cpart[tz, yy, :, k].astype(F32) + crecv[tz, yy].astype(F32)).astype(BF)
            return carry

        lax.fori_loop(0, 4, body, 0)
        for here, copy in c_parts(tz):
            if tz is zl:

                @pl.when(jnp.logical_not(here))
                def _():
                    copy.start()

                @pl.when(here)
                def _():
                    c_own.start()

            else:
                start(copy)

    narrow(0)
    pl.semaphore_wait(barrier, 49)
    u1_own.start()
    for dz in (2, 1, 3):
        start(u1(dz))
    own_in(0)
    narrow(1)
    narrow(2)
    own_in(1)
    p1_start(0)
    own_in(2)
    own_in(3)
    loads[3].wait()
    lax.fori_loop(0, 4, transpose_tokens, 0)
    start(tokens_pair(zl, k))
    x_relay(0)
    x_relay(1)
    pair_in(2)
    pair_in(3)
    p1_start(1)
    lax.fori_loop(0, 32, invert, 0)
    p1_wait(0)
    lax.fori_loop(0, 16, weights, 0)
    start(ring_w(y, 0, 128, g_up, 0), ring_w(y, 0, 128, g_dn, 1))
    pair_in(0)
    p1_start(2)
    pair_in(1)
    x_relay(2)
    x_relay(3)
    x_relay(6)
    x_relay(7)
    tokens_pair(zp, k).wait_recv()
    start(tokens_core(k))
    ring_w(y_dn, 0, 128, g_up, 0).wait_recv()
    start(ring_w(y_dn, 0, 64, g_up, 2))
    ring_w(y_up, 0, 128, g_dn, 1).wait_recv()
    start(ring_w(y_up, 64, 64, g_dn, 3))
    x_relay(4)
    x_relay(5)
    x_wait(0)
    x_wait(1)
    x_wait(6)
    x_wait(7)
    partial(zl)
    ring_w(y_far, 0, 64, g_up, 2).wait_recv()
    ring_w(y_far, 64, 64, g_dn, 3).wait_recv()
    back_send(zl)
    x_wait(2)
    x_wait(3)
    x_wait(4)
    x_wait(5)
    tokens_core(1 - k).wait_recv()
    partial(zp)
    sum_first(0)
    back_send(zp)
    back_sum(zl)
    sum_second(0)
    sum_first(1)
    p1_wait(1)
    p1_wait(2)
    back_sum(zp)
    adamw(0)
    p2_start(0)
    sum_second(1)
    adamw(1)
    p2_start(1)

    def c_wait(j, carry):
        remote(csum.at[0, 0, 0], cfin.at[j], cs.at[0, 0, 0], cr.at[j], g, t_core).wait_recv()
        return carry

    lax.fori_loop(0, 16, c_wait, 0)
    token = lax.broadcasted_iota(jnp.int32, (512, 128), 0)
    sums = []
    for xx in range(4):
        total = cfin[xx].astype(F32) + cfin[4 + xx].astype(F32)
        sums.append(total + cfin[8 + xx].astype(F32) + cfin[12 + xx].astype(F32))
    full = jnp.concatenate(sums, axis=0) * scale
    ig_ref[...] = jnp.where(token < live, full.T, 0.0).astype(BF)

    for i in range(NC):
        p2_own(i).wait()

        def p2_wait(j, carry):
            p2_in(i, j).wait_recv()
            p2(i, j).wait_send()
            return carry

        lax.fori_loop(1, 32, p2_wait, 0)

    for here, copy in c_parts(zl):

        @pl.when(jnp.logical_not(here))
        def _():
            copy.wait_send()


    def p1_sent(j, carry):
        for a in range(3):
            p1(a, j).wait_send()
        return carry

    lax.fori_loop(1, 32, p1_sent, 0)
    for c in sent:
        c.wait_send()


def shards(old_master, old_moment, old_second, tokens_in, upstream, counts, old_map, new_map):
    hbm = pl.BlockSpec(memory_space=pl.ANY)
    smem = pl.BlockSpec(memory_space=pltpu.SMEM)
    vmem = pl.BlockSpec(memory_space=pltpu.VMEM)
    dma = pltpu.SemaphoreType.DMA
    pieces, input_grad = pl.pallas_call(
        kernel,
        out_shape=(
            jax.ShapeDtypeStruct((3, 2, 4, 32, 1024), BF),
            jax.ShapeDtypeStruct((512, 128), BF),
        ),
        in_specs=[smem] * 3 + [hbm] * 5,
        out_specs=(vmem, vmem),
        scratch_shapes=[
            pltpu.SMEM((32,), jnp.int32),
            pltpu.VMEM((3, 128, 2048), F32),
            pltpu.VMEM((512, 4096), BF),
            pltpu.VMEM((3, 2, 4, 32, 1024), BF),
            pltpu.VMEM((32, 2, 32, 128), BF),
            pltpu.VMEM((32, 2, 32, 128), BF),
            pltpu.VMEM((32, 2, 32, 128), BF),
            pltpu.VMEM((1024, 2048), BF),
            pltpu.VMEM((512, 1024), BF),
            pltpu.VMEM((512, 512), BF),
            pltpu.VMEM((512, 2048), F32),
            pltpu.VMEM((512, 2048), BF),
            pltpu.VMEM((NC, 2, RR, 2048), BF),
            pltpu.VMEM((NC, 2, 2, RR, 2048), BF),
            pltpu.VMEM((512, 2048), BF),
            pltpu.VMEM((NC, 32, 3, RR, 128), BF),
            [pltpu.VMEM((32, 3, RR, 128), BF)] * NC,
            pltpu.VMEM((2, 4, 2, 2, 32, 512), CT),
            pltpu.VMEM((2, 4, 2, 32, 512), CT),
            pltpu.VMEM((2, 4, 2, 32, 512), BF),
            pltpu.VMEM((16, 32, 512), BF),
            dma((4,)), dma((4,)), dma((4,)), dma((4,)), dma((4,)), dma((2,)), dma((2,)),
            dma((3, 32)), dma((3, 32)), dma((8, 4)), dma((8, 4)), dma((4,)), dma((4,)),
            dma((NC, 6)), dma((NC, 6)), dma((NC, 32)), dma((NC, 32)),
            dma((2,)), dma((2,)), dma((2, 4, 2)), dma((16,)),
        ],
        compiler_params=pltpu.CompilerParams(
            collective_id=0, has_side_effects=True, vmem_limit_bytes=56 * 1024 * 1024
        ),
        cost_estimate=pl.CostEstimate(flops=4 * 2**30, bytes_accessed=12 * 2**20, transcendentals=2**18),
    )(
        old_map, new_map, counts,
        old_master.reshape(128, 2048), old_moment.reshape(128, 2048), old_second.reshape(128, 2048),
        tokens_in, upstream,
    )
    pieces = pieces.reshape(3, 1, 1, 256, 1024).astype(F32)
    return pieces[0], pieces[1], pieces[2], input_grad


def solution(mesh):
    pieces = P("tensor", "dp", None, None)
    return jax.shard_map(
        shards,
        mesh=mesh,
        in_specs=(pieces, pieces, pieces, P("dp", None), P("dp", "tensor"), P(), P(), P()),
        out_specs=(pieces, pieces, pieces, P("dp", "tensor")),
        check_vma=False,
    )
```

```python
import jax
import jax.numpy as jnp
from jax import lax
from jax.experimental import pallas as pl
from jax.experimental.pallas import tpu as pltpu
from jax.sharding import PartitionSpec as P

beta_first = 0.9
beta_second = 0.95
learn_rate = 0.05
decay_rate = 0.1
epsilon = 1e-08

BF = jnp.bfloat16
F32 = jnp.float32
NT = (((1,), (1,)), ((), ()))
NC = 2
PER = NC // 2
RR = 32 // PER
CT = F32


def kernel(
    map_ref, new_ref, cnt_ref, om_ref, oo_ref, os_ref, tok_ref, up_ref,
    out_ref, ig_ref,
    inv_ref, old, tok, send1, spread_a, spread_b, spread_c, gath, lhs, tsend, acc, part, r1, r2, wg,
    upd, send2, cpart, crecv, csum, cfin,
    ld, us, ur, es, er, ts, tr, p1s, p1r, xs, xr, ws, wr, rs, rr, p2s, p2r, ks, kr, cs, cr,
):
    spread = (spread_a, spread_b, spread_c)
    g = lax.axis_index("dp")
    t = lax.axis_index("tensor")
    zl, y = g // 4, g % 4
    z, x, k = t // 8, (t // 2) % 4, t % 2
    zp = 1 - zl
    y_up, y_dn, y_far = (y + 1) % 4, (y + 3) % 4, (y + 2) % 4
    g_up, g_dn, g_pair = zl * 4 + y_up, zl * 4 + y_dn, zp * 4 + y
    x_up, x_dn, x_far = (x + 1) % 4, (x + 3) % 4, (x + 2) % 4
    t_xup, t_xdn = z * 8 + x_up * 2 + k, z * 8 + x_dn * 2 + k
    t_core = z * 8 + x * 2 + 1 - k

    def remote(src, dst, ssem, rsem, dp, tn):
        return pltpu.make_async_remote_copy(
            src_ref=src, dst_ref=dst, send_sem=ssem, recv_sem=rsem,
            device_id=(dp, tn), device_id_type=pl.DeviceIdType.MESH,
        )

    def cols(index, width):
        return pl.ds(pl.multiple_of(index * width, width), width)

    def spread_out(n):
        return (n % 4) * 8 + n // 4

    sent = []

    def start(*copies):
        for c in copies:
            c.start()
            sent.append(c)

    loads = [
        pltpu.make_async_copy(src, old.at[a], ld.at[a]) for a, src in enumerate((om_ref, oo_ref, os_ref))
    ] + [pltpu.make_async_copy(tok_ref, tok, ld.at[3])]
    for c in loads:
        c.start()

    barrier = pltpu.get_barrier_semaphore()

    def greet(j, c):
        pl.semaphore_signal(barrier, inc=1, device_id=(g, (t + j) % 32), device_id_type=pl.DeviceIdType.MESH)
        return c

    lax.fori_loop(1, 32, greet, 0)
    for other in (g_up, g_dn):
        pl.semaphore_signal(barrier, inc=1, device_id=(other, t), device_id_type=pl.DeviceIdType.MESH)

    def greet_pair(j, c):
        pl.semaphore_signal(barrier, inc=1, device_id=(g_pair, j * 2 + k), device_id_type=pl.DeviceIdType.MESH)
        return c

    lax.fori_loop(0, 16, greet_pair, 0)

    def narrow(a):
        loads[a].wait()

        def body(i, c):
            c10, xx = i // 4, i % 4
            send1[a, c10, xx] = old[a, cols(xx, 32), cols(c10, 1024)].astype(BF)
            return c

        lax.fori_loop(0, 8, body, 0)

    near = 1 + 2 * zl
    z_near, z_other, z_far = (z + 4 - near) % 4, (z + near) % 4, (z + 2) % 4
    own_blocks = ((zl, z), (zl, z_near), (zp, z_near), (zp, z_far))
    pair_blocks = ((zp, z), (zp, z_other), (zl, z_other), (zl, z_far))

    def place_of(zz, zs, xx):
        return gath.at[cols(zz, 512), cols(xx * 4 + zs, 128)]

    def u1(dz):
        to = (z + dz) % 4
        lo, at = {1: (0, 1 + zl), 3: (1, 2 - zl), 2: (zp, 3)}[dz]
        return remote(
            up_ref.at[:, cols(to, 128)], place_of(zl, z, x), us.at[dz], ur.at[at], lo * 4 + y, to * 8 + x * 2 + k
        )

    def u1_in(n):
        return remote(up_ref.at[:, cols(z, 128)], place_of(*own_blocks[n], x), us.at[n], ur.at[n], g, t_core)

    u1_own = pltpu.make_async_copy(up_ref.at[:, cols(z, 128)], place_of(zl, z, x), ur.at[0])

    def u2(n):
        ref = place_of(*own_blocks[n], x)
        return remote(ref, ref, es.at[n], er.at[n], g_pair, t)

    def u2_in(n):
        ref = place_of(*pair_blocks[n], x)
        return remote(ref, ref, es.at[n], er.at[n], g_pair, t)

    def invert(piece, c):
        slot = jnp.int32(0)
        for s in range(1, 32):
            slot = jnp.where(map_ref[s] == piece, jnp.int32(s), slot)
        inv_ref[piece] = slot
        return c

    def p1(a, j):
        p = (t + j) % 32
        pz, px, pk = p // 8, (p // 2) % 4, p % 2
        return remote(
            send1.at[a, :, px, :, cols(pk * 4 + pz, 128)], spread[a].at[t],
            p1s.at[a, j], p1r.at[a, j], g, p,
        )

    def p1_in(a, j):
        return remote(
            send1.at[a, :, x, :, cols(k * 4 + z, 128)], spread[a].at[(t + 32 - j) % 32],
            p1s.at[a, j], p1r.at[a, j], g, t_core,
        )

    def p1_own(a):
        return pltpu.make_async_copy(send1.at[a, :, x, :, cols(k * 4 + z, 128)], spread[a].at[t], p1r.at[a, 0])

    def p1_start(a):
        p1_own(a).start()

        def body(n, c):
            p1(a, spread_out(n)).start()
            return c

        lax.fori_loop(1, 32, body, 0)

    def p1_wait(a):
        p1_own(a).wait()

        def body(j, c):
            p1_in(a, j).wait_recv()
            return c

        lax.fori_loop(1, 32, body, 0)

    live = cnt_ref[g]
    pick_row = lax.broadcasted_iota(jnp.int32, (128, 512), 0)
    pick_col = lax.broadcasted_iota(jnp.int32, (128, 512), 1)
    chunk_of, so1_of = pick_row // (2 * RR), (pick_row // RR) % 2
    so_of = so1_of * 2 + chunk_of // PER
    r_of = (chunk_of % PER) * RR + pick_row % RR
    pick = jnp.where(pick_col == so_of * 128 + x * 32 + r_of, 1.0, 0.0).astype(BF)
    alive = lax.broadcasted_iota(jnp.int32, (128, 512), 1) < live

    def transpose_tokens(yy, c):
        for zz, ref, where in ((zl, lhs, cols(zl, 512)), (zp, tsend, pl.ds(0, 512))):
            rows = lax.dot_general(pick, tok[:, cols(zz * 4 + yy, 512)], NT, preferred_element_type=F32)
            rows = jnp.where(alive, rows, 0.0).astype(BF)
            for i in range(NC):
                ref[cols(i * 4 + yy, 2 * RR), where] = rows[i * 2 * RR : (i + 1) * 2 * RR]
        return c

    def tokens_pair(zz, kk):
        rows = cols(kk, 256)
        return remote(tsend.at[rows], lhs.at[rows, cols(zz, 512)], ts.at[0], tr.at[0], g_pair, t)

    def tokens_core(kk):
        ref = lhs.at[cols(kk, 256), cols(zp, 512)]
        return remote(ref, ref, ts.at[1], tr.at[1], g, t_core)

    blocks = own_blocks + pair_blocks

    def x_copy(n, xx, rows, way, sem):
        zz, zs = blocks[n]
        ref = gath.at[pl.ds(pl.multiple_of(zz * 512 + rows[0], 256), rows[1]), cols(xx * 4 + zs, 128)]
        return remote(ref, ref, xs.at[n, sem], xr.at[n, sem], g, way)

    whole, top, bottom = (0, 512), (0, 256), (256, 256)

    def x_near(n):
        start(x_copy(n, x, whole, t_xup, 0), x_copy(n, x, whole, t_xdn, 1))

    def x_relay(n):
        x_copy(n, x_dn, whole, t_xup, 0).wait_recv()
        start(x_copy(n, x_dn, top, t_xup, 2))
        x_copy(n, x_up, whole, t_xdn, 1).wait_recv()
        start(x_copy(n, x_up, bottom, t_xdn, 3))

    def x_wait(n):
        x_copy(n, x_far, top, t_xup, 2).wait_recv()
        x_copy(n, x_far, bottom, t_xdn, 3).wait_recv()

    def own_in(n):
        if n == 0:
            u1_own.wait()
        else:
            u1_in(n).wait_recv()
        start(u2(n))
        x_near(n)

    def pair_in(n):
        u2_in(n).wait_recv()
        x_near(4 + n)

    def place(q):
        zs, half = q % 4, q // 4
        return zs * 2 + half // 2, half % 2

    def weights(q, c):
        bo, c10 = place(q)
        for so in range(4):
            wg[cols(y * 4 + so, 32), cols(q, 128)] = spread[0][inv_ref[bo * 4 + so], c10]
        return c

    def ring_w(yy, start_row, rows, to, sem):
        ref = wg.at[pl.ds(pl.multiple_of(yy * 128 + start_row, 64), rows), :]
        return remote(ref, ref, ws.at[sem], wr.at[sem], to, t)

    def block(i, yy, so1):
        return part.at[cols(i * 8 + yy * 2 + so1, RR), :]

    def partial(zz):
        def body(c, carry):
            here = cols(c, 512)
            product = jnp.dot(
                lhs[:, cols(zz, 512)], gath[cols(zz, 512), here], preferred_element_type=F32
            )
            if zz is zl:
                acc[:, here] = product
            else:
                part[:, here] = (acc[:, here] + product).astype(BF)
            return carry

        lax.fori_loop(0, 4, body, 0)

    def sum_copy(i, n, src, dst, to):
        return remote(src, dst, rs.at[i, n], rr.at[i, n], to, t)

    def far_up(i):
        return sum_copy(i, 0, block(i, y_far, 0), r1.at[i, 0], g_up)

    def far_dn(i):
        return sum_copy(i, 1, block(i, y_far, 1), r1.at[i, 1], g_dn)

    def near_up(i, so1):
        return sum_copy(i, 2 + so1, block(i, y_up, so1), r2.at[i, 0, so1], g_up)

    def near_dn(i, so1):
        return sum_copy(i, 4 + so1, block(i, y_dn, so1), r2.at[i, 1, so1], g_dn)

    def add_into(i, yy, so1):
        at = cols(i * 8 + yy * 2 + so1, RR)
        part[at, :] = (part[at, :].astype(F32) + r1[i, so1].astype(F32)).astype(BF)

    def sum_first(i):
        start(far_up(i), far_dn(i), near_up(i, 1), near_dn(i, 0))

    def sum_second(i):
        far_up(i).wait_recv()
        add_into(i, y_up, 0)
        start(near_up(i, 0))
        far_dn(i).wait_recv()
        add_into(i, y_dn, 1)
        start(near_dn(i, 1))

    fix_first = 1.0 - beta_first**10
    fix_second = 1.0 - beta_second**10
    scale = 1.0 / 64.0

    def adamw(i):
        for so1 in range(2):
            near_up(i, so1).wait_recv()
            near_dn(i, so1).wait_recv()
        so0, r0 = i // PER, (i % PER) * RR

        def body(zs, carry):
            done = []
            for xs in range(4):
                bo, c10 = zs * 2 + xs // 2, xs % 2
                here = cols(xs * 4 + zs, 128)
                for so1 in range(2):
                    slot = inv_ref[bo * 4 + so1 * 2 + so0]
                    mine = cols(i * 8 + y * 2 + so1, RR)
                    grad = part[mine, here].astype(F32) + r2[i, 0, so1, :, here].astype(F32)
                    grad = (grad + r2[i, 1, so1, :, here].astype(F32)) * scale
                    rows = slice(r0, r0 + RR)
                    master = spread[0][slot, c10, rows].astype(F32)
                    moment = beta_first * spread[1][slot, c10, rows].astype(F32) + (1.0 - beta_first) * grad
                    second = beta_second * spread[2][slot, c10, rows].astype(F32) + (1.0 - beta_second) * grad * grad
                    root = jnp.sqrt(second * (1.0 / fix_second)) + epsilon
                    update = moment * (1.0 / fix_first) / root + decay_rate * master
                    piece = (bo * 2 + c10) * 2 + so1
                    done.append((piece, master - learn_rate * update, moment, second))
            for piece, *values in done:
                for a, value in enumerate(values):
                    upd[i, piece, a] = value.astype(BF)
            return carry

        lax.fori_loop(0, 4, body, 0)

    def p2_place(i, px, pk, pz):
        return out_ref.at[:, i // PER, px, pl.ds((i % PER) * RR, RR), cols(pk * 4 + pz, 128)]

    def p2(i, j):
        p = (t + j) % 32
        return remote(send2[i].at[p], p2_place(i, x, k, z), p2s.at[i, j], p2r.at[i, j], g, p)

    def p2_in(i, j):
        p = (t + 32 - j) % 32
        return remote(
            send2[i].at[t], p2_place(i, (p // 2) % 4, p % 2, p // 8), p2s.at[i, j], p2r.at[i, j], g, t_core
        )

    def p2_own(i):
        return pltpu.make_async_copy(send2[i].at[t], p2_place(i, x, k, z), p2r.at[i, 0])

    def p2_start(i):
        def select(j, carry):
            for u in range(4):
                send2[i][j * 4 + u] = upd[i, new_ref[j * 4 + u]]
            return carry

        lax.fori_loop(0, 8, select, 0)

        def body(n, carry):
            p2(i, spread_out(n)).start()
            return carry

        lax.fori_loop(1, 32, body, 0)
        p2_own(i).start()

    def back(tz):
        def body(c, carry):
            rows = lax.dot_general(
                wg[...], gath[cols(tz * 2 + c, 256), :], NT, preferred_element_type=F32
            )
            for yy in range(4):
                for so in range(4):
                    at = yy * 128 + so * 32
                    cpart[tz, yy, so // 2, so % 2, :, cols(c, 256)] = rows[at : at + 32].astype(CT)
            return carry

        lax.fori_loop(0, 2, body, 0)

    def core_copy(tz):
        at = 0 if tz is zl else 1
        return remote(cpart.at[tz, :, :, 1 - k], crecv.at[tz], ks.at[at], kr.at[at], g, t_core)

    def back_send(tz):
        back(tz)
        start(core_copy(tz))

    me16 = z * 4 + x
    c_own = pltpu.make_async_copy(csum.at[zl, (z % 2) * 2 + x // 2, x % 2], cfin.at[me16], cr.at[me16])

    def c_parts(tz):
        for yy in range(4):
            for so1 in range(2):
                pz, px = zl * 2 + yy // 2, (yy % 2) * 2 + so1
                here = jnp.logical_and(pz == z, px == x)
                copy = remote(
                    csum.at[tz, yy, so1], cfin.at[me16], cs.at[0 if tz is zl else 1, yy, so1], cr.at[me16],
                    tz * 4 + y, pz * 8 + px * 2 + k,
                )
                yield here, copy

    def back_sum(tz):
        core_copy(tz).wait_recv()

        def body(yy, carry):
            csum[tz, yy] = (cpart[tz, yy, :, k].astype(F32) + crecv[tz, yy].astype(F32)).astype(BF)
            return carry

        lax.fori_loop(0, 4, body, 0)
        for here, copy in c_parts(tz):
            if tz is zl:

                @pl.when(jnp.logical_not(here))
                def _():
                    copy.start()

                @pl.when(here)
                def _():
                    c_own.start()

            else:
                start(copy)

    narrow(0)
    pl.semaphore_wait(barrier, 49)
    u1_own.start()
    for dz in (2, 1, 3):
        start(u1(dz))
    own_in(0)
    narrow(1)
    narrow(2)
    own_in(1)
    p1_start(0)
    own_in(2)
    own_in(3)
    loads[3].wait()
    lax.fori_loop(0, 4, transpose_tokens, 0)
    start(tokens_pair(zl, k))
    x_relay(0)
    x_relay(1)
    pair_in(2)
    pair_in(3)
    p1_start(1)
    lax.fori_loop(0, 32, invert, 0)
    p1_wait(0)
    lax.fori_loop(0, 16, weights, 0)
    start(ring_w(y, 0, 128, g_up, 0), ring_w(y, 0, 128, g_dn, 1))
    pair_in(0)
    pair_in(1)
    p1_start(2)
    x_relay(2)
    x_relay(3)
    x_relay(6)
    x_relay(7)
    tokens_pair(zp, k).wait_recv()
    start(tokens_core(k))
    ring_w(y_dn, 0, 128, g_up, 0).wait_recv()
    start(ring_w(y_dn, 0, 64, g_up, 2))
    ring_w(y_up, 0, 128, g_dn, 1).wait_recv()
    start(ring_w(y_up, 64, 64, g_dn, 3))
    x_relay(4)
    x_relay(5)
    x_wait(0)
    x_wait(1)
    x_wait(6)
    x_wait(7)
    partial(zl)
    ring_w(y_far, 0, 64, g_up, 2).wait_recv()
    ring_w(y_far, 64, 64, g_dn, 3).wait_recv()
    back_send(zl)
    x_wait(2)
    x_wait(3)
    x_wait(4)
    x_wait(5)
    tokens_core(1 - k).wait_recv()
    partial(zp)
    sum_first(0)
    back_send(zp)
    back_sum(zl)
    sum_second(0)
    sum_first(1)
    p1_wait(1)
    p1_wait(2)
    back_sum(zp)
    adamw(0)
    p2_start(0)
    sum_second(1)
    adamw(1)
    p2_start(1)

    def c_wait(j, carry):
        remote(csum.at[0, 0, 0], cfin.at[j], cs.at[0, 0, 0], cr.at[j], g, t_core).wait_recv()
        return carry

    lax.fori_loop(0, 16, c_wait, 0)
    token = lax.broadcasted_iota(jnp.int32, (512, 128), 0)
    sums = []
    for xx in range(4):
        total = cfin[xx].astype(F32) + cfin[4 + xx].astype(F32)
        sums.append(total + cfin[8 + xx].astype(F32) + cfin[12 + xx].astype(F32))
    full = jnp.concatenate(sums, axis=0) * scale
    ig_ref[...] = jnp.where(token < live, full.T, 0.0).astype(BF)

    for i in range(NC):
        p2_own(i).wait()

        def p2_wait(j, carry):
            p2_in(i, j).wait_recv()
            p2(i, j).wait_send()
            return carry

        lax.fori_loop(1, 32, p2_wait, 0)

    for here, copy in c_parts(zl):

        @pl.when(jnp.logical_not(here))
        def _():
            copy.wait_send()


    def p1_sent(j, carry):
        for a in range(3):
            p1(a, j).wait_send()
        return carry

    lax.fori_loop(1, 32, p1_sent, 0)
    for c in sent:
        c.wait_send()


def shards(old_master, old_moment, old_second, tokens_in, upstream, counts, old_map, new_map):
    hbm = pl.BlockSpec(memory_space=pl.ANY)
    smem = pl.BlockSpec(memory_space=pltpu.SMEM)
    vmem = pl.BlockSpec(memory_space=pltpu.VMEM)
    dma = pltpu.SemaphoreType.DMA
    pieces, input_grad = pl.pallas_call(
        kernel,
        out_shape=(
            jax.ShapeDtypeStruct((3, 2, 4, 32, 1024), BF),
            jax.ShapeDtypeStruct((512, 128), BF),
        ),
        in_specs=[smem] * 3 + [hbm] * 5,
        out_specs=(vmem, vmem),
        scratch_shapes=[
            pltpu.SMEM((32,), jnp.int32),
            pltpu.VMEM((3, 128, 2048), F32),
            pltpu.VMEM((512, 4096), BF),
            pltpu.VMEM((3, 2, 4, 32, 1024), BF),
            pltpu.VMEM((32, 2, 32, 128), BF),
            pltpu.VMEM((32, 2, 32, 128), BF),
            pltpu.VMEM((32, 2, 32, 128), BF),
            pltpu.VMEM((1024, 2048), BF),
            pltpu.VMEM((512, 1024), BF),
            pltpu.VMEM((512, 512), BF),
            pltpu.VMEM((512, 2048), F32),
            pltpu.VMEM((512, 2048), BF),
            pltpu.VMEM((NC, 2, RR, 2048), BF),
            pltpu.VMEM((NC, 2, 2, RR, 2048), BF),
            pltpu.VMEM((512, 2048), BF),
            pltpu.VMEM((NC, 32, 3, RR, 128), BF),
            [pltpu.VMEM((32, 3, RR, 128), BF)] * NC,
            pltpu.VMEM((2, 4, 2, 2, 32, 512), CT),
            pltpu.VMEM((2, 4, 2, 32, 512), CT),
            pltpu.VMEM((2, 4, 2, 32, 512), BF),
            pltpu.VMEM((16, 32, 512), BF),
            dma((4,)), dma((4,)), dma((4,)), dma((4,)), dma((4,)), dma((2,)), dma((2,)),
            dma((3, 32)), dma((3, 32)), dma((8, 4)), dma((8, 4)), dma((4,)), dma((4,)),
            dma((NC, 6)), dma((NC, 6)), dma((NC, 32)), dma((NC, 32)),
            dma((2,)), dma((2,)), dma((2, 4, 2)), dma((16,)),
        ],
        compiler_params=pltpu.CompilerParams(
            collective_id=0, has_side_effects=True, vmem_limit_bytes=56 * 1024 * 1024
        ),
        cost_estimate=pl.CostEstimate(flops=4 * 2**30, bytes_accessed=12 * 2**20, transcendentals=2**18),
    )(
        old_map, new_map, counts,
        old_master.reshape(128, 2048), old_moment.reshape(128, 2048), old_second.reshape(128, 2048),
        tokens_in, upstream,
    )
    pieces = pieces.reshape(3, 1, 1, 256, 1024).astype(F32)
    return pieces[0], pieces[1], pieces[2], input_grad


def solution(mesh):
    pieces = P("tensor", "dp", None, None)
    return jax.shard_map(
        shards,
        mesh=mesh,
        in_specs=(pieces, pieces, pieces, P("dp", None), P("dp", "tensor"), P(), P(), P()),
        out_specs=(pieces, pieces, pieces, P("dp", "tensor")),
        check_vma=False,
    )
```
